128 devices in a mesh: gx: 8 (over z, x_lo), gy: 16 (over y, x_hi, core).
Axes of the slice: x: 4 (x_hi: 2, x_lo: 2; x = x_hi * 2 + x_lo), y: 4, z: 4, core: 2. Of those that a mesh axis runs over, the one named last changes fastest.
Arguments:
- features: bfloat16 [8, 16, 2, 16, 16, 1024], P('gx', 'gy'), may hold values from -6 to 6
- mask: int32 [8, 16, 2, 16, 16, 16], P('gx', 'gy'), may hold values from 0 to 1, as said below
- labels: int32 [8, 16, 2, 16, 16, 16], P('gx', 'gy'), may hold values from 0 to 2
- kernel_map: int32 [8, 16, 2, 27], P('gx', 'gy'), may hold values from -1 to 1, as said below
- weight: bfloat16 [27, 64, 64], replicated, may hold values from -0.15625 to 0.15625
- classifier: bfloat16 [3, 64], replicated, may hold values from -0.75 to 0.75
Outputs:
- grad_input: bfloat16 [8, 16, 2, 16, 16, 1024], P('gx', 'gy')
- weight_grad: float32 [27, 64, 64], replicated
- classifier_grad: float32 [3, 64], replicated
The draws below stay inside these ranges and needn't reach their ends.
Inputs may be any that keep to these rules, and one draw needn't show every extreme that they name: `mask`: Occupancy: 1 for occupied voxels of an active block; every voxel of an empty slot is 0. The active slots of a column are its first ones, 1 to 2 of them, and some column has all 2 active. `kernel_map`: entry [i, j, t, o] is the slot of column (i + a, j + b) holding the active block at offset (a, b, c) from the block in slot t, or -1 if there is none or slot t is empty. The blocks of one column sit at distinct positions among 8 along z, so each active block has at most one source for each offset; offset 13 of an active slot t is t itself.
All inputs are finite; a program needn't handle non-finite values.
Results may differ from the reference program's by a relative error of at most 0.015.
Values may be sent and summed in bfloat16 or wider, within the bound.
A program may use at most 192 MiB of HBM per device.

```python
import jax
import jax.numpy as jnp
from jax import lax

C = 64
BS = 16
KINDS = 3
SLOTS = 2
RZ = 8
COLS_X = 8
COLS_Y = 16


def layout(key):
    place_key = jax.random.fold_in(key, 101)
    count_key = jax.random.fold_in(key, 102)
    full_key = jax.random.fold_in(key, 103)
    columns = COLS_X * COLS_Y
    keys = jax.random.split(place_key, columns)
    places = jax.vmap(lambda single: jax.random.permutation(single, RZ)[:SLOTS])(keys).astype(jnp.int32)
    counts = jax.random.randint(count_key, (columns,), 1, SLOTS + 1)
    fullest = jax.random.randint(full_key, (), 0, columns)
    counts = jnp.where(jnp.arange(columns) == fullest, SLOTS, counts)
    active = jnp.arange(SLOTS)[None, :] < counts[:, None]
    codes = jnp.where(active, places + 1, 0)
    return codes.reshape(COLS_X, COLS_Y, SLOTS).astype(jnp.int32)


def draw_mask(key, part):
    codes = layout(key)
    key = jax.random.fold_in(key, 11)
    density_key, roll_key = jax.random.split(key)
    density = jax.random.randint(density_key, (COLS_X, COLS_Y, SLOTS, 1, 1, 1), 40, 96)
    rolls = jax.random.randint(roll_key, (COLS_X, COLS_Y, SLOTS, BS, BS, BS), 0, 100)
    voxel = (rolls < density) & (codes[:, :, :, None, None, None] > 0)
    return voxel.astype(jnp.int32)


def draw_kernel_map(key, part):
    codes = layout(key)
    padded = jnp.pad(codes, ((1, 1), (1, 1), (0, 0)))
    slot_ids = jnp.arange(SLOTS, dtype=jnp.int32)[None, None, None, :] + 1
    columns = []
    for a in (-1, 0, 1):
        for b in (-1, 0, 1):
            for c in (-1, 0, 1):
                beside = padded[1 + a:1 + a + COLS_X, 1 + b:1 + b + COLS_Y]
                hit = (beside[:, :, None, :] == codes[:, :, :, None] + c) & (codes[:, :, :, None] > 0) & (beside[:, :, None, :] > 0)
                columns.append(jnp.sum(jnp.where(hit, slot_ids, 0), axis=3) - 1)
    return jnp.stack(columns, axis=-1).astype(jnp.int32)


def plant(drawn, own_key, low, largest):
    extent = drawn.shape
    spot = [jax.random.randint(jax.random.fold_in(own_key, axis), (), 0, extent[axis]) for axis in range(len(extent))]
    drawn = drawn.at[tuple(spot)].set(low)
    longest = extent.index(max(extent))
    spot[longest] = (spot[longest] + 1) % extent[longest]
    return drawn.at[tuple(spot)].set(largest)


def block_scale(key, shape, cuts, least, largest):
    gain, own = 1.0, jax.random.fold_in(key, 6)
    for dim, parts in cuts:
        steps = jnp.exp(jax.random.uniform(jax.random.fold_in(own, dim), (parts,), jnp.float32, least / len(cuts), largest / len(cuts)))
        gain = gain * jnp.repeat(steps, shape[dim] // parts).reshape([-1 if axis == dim else 1 for axis in range(len(shape))])
    return gain


def noise(stream_key, dims, scale, reach, cuts=(), held_as=jnp.bfloat16):
    values = jax.random.normal(stream_key, dims, jnp.float32) * scale
    if len(cuts) > 0:
        values = block_scale(stream_key, dims, cuts, -0.22, 0.18) * values
    return jnp.clip(values, min=-reach, max=reach).astype(held_as)


def setup_inputs(seed: int = 0) -> dict:
    arg_keys = jax.random.split(jax.random.key(seed), 7)
    features = noise(arg_keys[0], (COLS_X, COLS_Y, SLOTS, BS, BS, BS * C), 1.0, 6.0, ((0, 8), (1, 16)))
    mask = draw_mask(jax.random.fold_in(arg_keys[6], 71), 0)
    labels = plant(jax.random.randint(arg_keys[2], (COLS_X, COLS_Y, SLOTS, BS, BS, BS), 0, KINDS), jax.random.fold_in(arg_keys[2], 1), 0, KINDS - 1).astype(jnp.int32)
    kernel_map = draw_kernel_map(jax.random.fold_in(arg_keys[6], 71), 0)
    weight = noise(arg_keys[4], (27, C, C), (27 * C) ** -0.5, 0.15625)
    classifier = noise(arg_keys[5], (KINDS, C), C ** -0.5, 0.75)
    return dict(features=features, mask=mask, labels=labels, kernel_map=kernel_map, weight=weight, classifier=classifier)


def offset_list():
    return [(a, b, c) for a in (-1, 0, 1) for b in (-1, 0, 1) for c in (-1, 0, 1)]


def span_cut(shift, side):
    if shift == -1:
        return slice(side - 1, side)
    if shift == 0:
        return slice(0, side)
    return slice(0, 1)


def depth_cut(block, shift, side, channels):
    if shift == -1:
        return block[..., (side - 1) * channels:]
    if shift == 0:
        return block
    return block[..., :channels]


def select_piece(column, piece):
    hits = (column[:, None] == jnp.arange(piece.shape[0], dtype=jnp.int32)[None, :]).astype(jnp.float32)
    picked = jnp.einsum("ts,sxyz->txyz", hits, piece.astype(jnp.float32))
    return picked.astype(piece.dtype)


def assemble(own, neighbours, dev_map, side, channels):
    layers = []
    for a in (-1, 0, 1):
        columns = []
        for b in (-1, 0, 1):
            source = own if (a == 0 and b == 0) else neighbours[(a, b)]
            pieces = []
            for c in (-1, 0, 1):
                offset_id = (a + 1) * 9 + (b + 1) * 3 + (c + 1)
                pieces.append(select_piece(dev_map[:, offset_id], depth_cut(source, c, side, channels)))
            columns.append(jnp.concatenate(pieces, axis=3))
        layers.append(jnp.concatenate(columns, axis=2))
    return jnp.concatenate(layers, axis=1)


def convolve(padded, weights, flip, side, channels):
    count = padded.shape[0]
    total = jnp.zeros((count * side ** 3, channels), jnp.float32)
    sign = -1 if flip else 1
    for offset_id, (a, b, c) in enumerate(offset_list()):
        start_x, start_y, start_z = 1 + sign * a, 1 + sign * b, 1 + sign * c
        slab = padded[:, start_x:start_x + side, start_y:start_y + side, start_z * channels:(start_z + side) * channels]
        matrix = weights[offset_id].T if flip else weights[offset_id]
        total = total + jnp.dot(slab.reshape(-1, channels).astype(jnp.float32), matrix.astype(jnp.float32))
    return total.reshape(count, side, side, side * channels)


def weight_terms(padded, grad_pre, side, channels):
    flat_grad = grad_pre.reshape(-1, channels).astype(jnp.float32)
    terms = []
    for a, b, c in offset_list():
        slab = padded[:, 1 + a:1 + a + side, 1 + b:1 + b + side, (1 + c) * channels:(1 + c + side) * channels]
        terms.append(jnp.einsum("vc,vd->cd", slab.reshape(-1, channels).astype(jnp.float32), flat_grad))
    return jnp.stack(terms)


def spread_mask(dev_mask, channels):
    shape = dev_mask.shape
    wide = jnp.broadcast_to(dev_mask[..., None], shape + (channels,))
    return wide.reshape(shape[:-1] + (shape[-1] * channels,))


def forward_backward(padded, dev_mask, dev_labels, weights, classifier, side, channels):
    pre = convolve(padded, weights, False, side, channels)
    voxel_on = spread_mask(dev_mask, channels).astype(jnp.float32)
    sigmoid_pre = jax.nn.sigmoid(pre)
    hidden = (pre * sigmoid_pre * voxel_on).astype(jnp.bfloat16)
    flat_hidden = hidden.reshape(-1, channels).astype(jnp.float32)
    logits = jnp.einsum("kc,vc->kv", classifier.astype(jnp.float32), flat_hidden)
    expo = jnp.exp(logits)
    prob = expo / jnp.sum(expo, axis=0, keepdims=True)
    kinds = classifier.shape[0]
    target = (dev_labels.reshape(1, -1) == jnp.arange(kinds, dtype=jnp.int32)[:, None]).astype(jnp.float32)
    voxel_flat = dev_mask.reshape(1, -1).astype(jnp.float32)
    grad_logits = ((prob - target) * voxel_flat).astype(jnp.bfloat16).astype(jnp.float32)
    class_part = jnp.einsum("kv,vc->kc", grad_logits, flat_hidden)
    grad_hidden = jnp.einsum("kv,kc->vc", grad_logits, classifier.astype(jnp.float32)).reshape(pre.shape)
    grad_pre = (grad_hidden * sigmoid_pre * (1.0 + pre * (1.0 - sigmoid_pre)) * voxel_on).astype(jnp.bfloat16)
    weight_part = weight_terms(padded, grad_pre, side, channels)
    return grad_pre, weight_part, class_part


def neighbour_blocks(neigh, side):
    result = {}
    for a in (-1, 0, 1):
        for b in (-1, 0, 1):
            if a != 0 or b != 0:
                result[(a, b)] = neigh[1 + a, 1 + b][:, span_cut(a, side), span_cut(b, side)]
    return result


def reference(features, mask, labels, kernel_map, weight, classifier):
    grid_x, grid_y = features.shape[0], features.shape[1]
    count = grid_x * grid_y
    masked = features * spread_mask(mask, C).astype(features.dtype)
    pad_width = ((1, 1), (1, 1), (0, 0), (0, 0), (0, 0), (0, 0))
    padded_in = jnp.pad(masked, pad_width)
    places = jnp.arange(count, dtype=jnp.int32)
    flat_masks = mask.reshape((count, SLOTS, BS, BS, BS))
    flat_labels = labels.reshape((count, SLOTS, BS, BS, BS))
    flat_maps = kernel_map.reshape((count, SLOTS, 27))
    zero = jnp.zeros((), jnp.int32)
    window = (3, 3, SLOTS, BS, BS, BS * C)

    def first_pass(items):
        place, dev_mask, dev_labels, dev_map = items
        row_id = (place // grid_y).astype(jnp.int32)
        col_id = (place % grid_y).astype(jnp.int32)
        neigh = lax.dynamic_slice(padded_in, (row_id, col_id, zero, zero, zero, zero), window)
        padded = assemble(neigh[1, 1], neighbour_blocks(neigh, BS), dev_map, BS, C)
        return forward_backward(padded, dev_mask, dev_labels, weight, classifier, BS, C)

    grad_pre, weight_parts, class_parts = lax.map(first_pass, (places, flat_masks, flat_labels, flat_maps))
    scale = float(count * SLOTS * BS ** 3) ** -0.5
    weight_grad = jnp.sum(weight_parts, axis=0) * scale
    classifier_grad = jnp.sum(class_parts, axis=0) * scale
    padded_grad = jnp.pad(grad_pre.reshape(features.shape), pad_width)

    def second_pass(items):
        place, dev_mask, dev_map = items
        row_id = (place // grid_y).astype(jnp.int32)
        col_id = (place % grid_y).astype(jnp.int32)
        neigh = lax.dynamic_slice(padded_grad, (row_id, col_id, zero, zero, zero, zero), window)
        padded = assemble(neigh[1, 1], neighbour_blocks(neigh, BS), dev_map, BS, C)
        grad = convolve(padded, weight, True, BS, C)
        return (grad * spread_mask(dev_mask, C).astype(jnp.float32)).astype(jnp.bfloat16)

    grad_input = lax.map(second_pass, (places, flat_masks, flat_maps)).reshape(features.shape)
    return grad_input, weight_grad, classifier_grad
```

```python
import jax
import jax.numpy as jnp
from jax import lax
from jax.experimental import pallas as pl
from jax.experimental.pallas import tpu as pltpu
from jax.sharding import PartitionSpec as P

MESH = pl.DeviceIdType.MESH
F32, BF16, I32 = jnp.float32, jnp.bfloat16, jnp.int32
NX, NY = 8, 16
CHUNKS = 14
DIRS = [(a, b) for a in (-1, 0, 1) for b in (-1, 0, 1) if (a, b) != (0, 0)]
XD = [(-1, 0), (1, 0)]
YD = [(0, -1), (0, 1)]
CD = [(-1, -1), (-1, 1), (1, -1), (1, 1)]


def iota(shape, dim):
    return lax.broadcasted_iota(I32, shape, dim)


def dot(a, b):
    return jnp.dot(a, b, preferred_element_type=F32)


def dot_t(a, b):
    return lax.dot_general(a, b, (((1,), (1,)), ((), ())), preferred_element_type=F32)


def tdot(a, b):
    return lax.dot_general(a, b, (((0,), (0,)), ((), ())), preferred_element_type=F32)


def one_hot(cond):
    return jnp.where(cond, 1.0, 0.0).astype(BF16)


def pick(m, first, second):
    return jnp.where(m == 0, first, jnp.where(m == 1, second, 0.0))


def low_half(rows):
    return iota((rows, 128), 1) < 64


def swap(x):
    return pltpu.roll(x, 64, axis=1)


def deepen(before, body, after):
    tiles = [before] + body + [after]
    low = low_half(before.shape[0])
    return [swap(jnp.where(low, tiles[k + 1], tiles[k])) for k in range(9)]


def offset_id(a, b, c):
    return (a + 1) * 9 + (b + 1) * 3 + (c + 1)


class Halo:
    def __init__(self, src, ysend, csend, corner, rx, ry, rc, send_sem, recv_sem, base, gx, gy):
        self.src, self.ysend, self.csend, self.corner = src, ysend, csend, corner
        self.rx, self.ry, self.rc = rx, ry, rc
        self.send_sem, self.recv_sem, self.base = send_sem, recv_sem, base
        self.gx, self.gy = gx, gy

    def prepare(self):
        r = iota((32, 256), 0)
        c = iota((32, 256), 1)
        sel = one_hot(c == (r & 15) * 16 + (r >> 4) * 15)
        for s in range(2):
            rows = dot(sel, self.src[s])
            self.ysend[0, s] = rows[:16].astype(BF16)
            self.ysend[1, s] = rows[16:].astype(BF16)
            for n, (a, b) in enumerate(CD):
                at = (16 if b > 0 else 0) + (15 if a > 0 else 0)
                for k in range(8):
                    self.corner[n, s * 8 + k : s * 8 + k + 1, :] = rows[at : at + 1, k * 128 : (k + 1) * 128]
        for n in range(4):
            self.csend[n] = self.corner[n].astype(BF16)

    def copies(self):
        out = []
        for n, (a, b) in enumerate(XD + YD + CD):
            if n < 2:
                src, dst, opp = self.src.at[:, pl.ds(15 * 16 if a > 0 else 0, 16), :], self.rx.at[1 - n], 1 - n
            elif n < 4:
                src, dst, opp = self.ysend.at[n - 2], self.ry.at[3 - n], 5 - n
            else:
                src, dst, opp = self.csend.at[n - 4], self.rc.at[7 - n], 11 - n
            to = (lax.rem(self.gx + a + NX, NX), lax.rem(self.gy + b + NY, NY))
            out.append(
                pltpu.make_async_remote_copy(
                    src_ref=src,
                    dst_ref=dst,
                    send_sem=self.send_sem.at[self.base + n],
                    recv_sem=self.recv_sem.at[self.base + opp],
                    device_id=to,
                    device_id_type=MESH,
                )
            )
        return out


def split_tiles(x):
    return [x[:, k * 128 : (k + 1) * 128] for k in range(x.shape[1] // 128)]


def build_padded(halo, kmap, pad, edge):
    src = halo.src
    for e, b in enumerate((-1, 1)):
        for s in range(2):
            one, two = halo.ry[e, 0].astype(F32), halo.ry[e, 1].astype(F32)
            m = [kmap[s, offset_id(0, b, c)] for c in (-1, 0, 1)]
            tiles = deepen(
                pick(m[0], one[:, 896:], two[:, 896:]),
                split_tiles(pick(m[1], one, two)),
                pick(m[2], one[:, :128], two[:, :128]),
            )
            edge[e, s, 0:16, :] = jnp.concatenate(tiles, axis=1)
            for w, a in enumerate((-1, 1)):
                packed = halo.rc[CD.index((a, b))].astype(F32)
                m = [kmap[s, offset_id(a, b, c)] for c in (-1, 0, 1)]
                before, mid, after = (pick(v, packed[:8], packed[8:]) for v in m)
                low = low_half(8)
                first = iota((8, 128), 0) == 0
                prev = pltpu.roll(jnp.where(iota((8, 128), 0) == 7, before, mid), 1, axis=0)
                body = swap(jnp.where(low, mid, prev))
                last = swap(jnp.where(low, pltpu.roll(after, 7, axis=0), mid))
                del first
                for k in range(8):
                    edge[e, s, 16 + w : 17 + w, k * 128 : (k + 1) * 128] = body[k : k + 1]
                edge[e, s, 16 + w : 17 + w, 1024:1152] = last[7:8]

    def put(s, plane, row, tiles):
        at = pl.multiple_of(plane * 16, 16)
        top = iota((16, 128), 0) == 0
        end = iota((16, 128), 0) == 15
        lo = edge[0, s, pl.ds(row, 1), :]
        hi = edge[1, s, pl.ds(row, 1), :]
        for k in range(9):
            lanes = slice(k * 128, (k + 1) * 128)
            t = tiles[k]
            pad[1, s, pl.ds(at, 16), lanes] = t.astype(BF16)
            pad[0, s, pl.ds(at, 16), lanes] = jnp.where(top, lo[:, lanes], pltpu.roll(t, 1, axis=0)).astype(BF16)
            pad[2, s, pl.ds(at, 16), lanes] = jnp.where(end, hi[:, lanes], pltpu.roll(t, 15, axis=0)).astype(BF16)

    for s in range(2):
        for w, a in enumerate((-1, 1)):
            one, two = halo.rx[w, 0].astype(F32), halo.rx[w, 1].astype(F32)
            m = [kmap[s, offset_id(a, 0, c)] for c in (-1, 0, 1)]
            tiles = deepen(
                pick(m[0], one[:, 896:], two[:, 896:]),
                split_tiles(pick(m[1], one, two)),
                pick(m[2], one[:, :128], two[:, :128]),
            )
            put(s, 17 * w, 16 + w, tiles)
        down, up = kmap[s, 12], kmap[s, 14]

        def plane(x, carry):
            at = pl.multiple_of(x * 16, 16)
            own = src[s, pl.ds(at, 16), :].astype(F32)
            before = pick(down, src[0, pl.ds(at, 16), 896:1024].astype(F32), src[1, pl.ds(at, 16), 896:1024].astype(F32))
            after = pick(up, src[0, pl.ds(at, 16), 0:128].astype(F32), src[1, pl.ds(at, 16), 0:128].astype(F32))
            put(s, x + 1, x, deepen(before, split_tiles(own), after))
            return carry

        lax.fori_loop(0, 16, plane, 0)


def conv(pad, band, s, q):
    lanes = pl.ds(pl.multiple_of(q * 256, 256), 384)
    pieces = [pad[dy, s, pl.ds(dx * 16, 256), lanes] for dx in range(3) for dy in range(3)]
    return dot(jnp.concatenate(pieces, axis=1), band[...])


def build_bands(wt, band, flip):
    dup = one_hot((iota((64, 128), 1) & 63) == iota((64, 128), 0))
    low = low_half(64)
    zero = jnp.zeros((64, 128), F32)

    def group(g, carry):
        fore = dot(wt[pl.ds(pl.multiple_of(g * 192, 64), 192), :], dup)
        parts = [fore[d * 64 : (d + 1) * 64] for d in range(3)]
        back = [tdot(wt[pl.ds(pl.multiple_of((8 - g) * 192 + (2 - d) * 64, 64), 64), :], dup) for d in range(3)]
        for which, ref in ((parts, band), (back, flip)):
            for i in range(6):
                for t in range(2):
                    a, b = i - 2 * t, i - 2 * t - 1
                    x = jnp.where(low, which[a] if 0 <= a < 3 else zero, which[b] if 0 <= b < 3 else zero)
                    at = pl.multiple_of(g * 384 + i * 64, 64)
                    ref[pl.ds(at, 64), t * 128 : (t + 1) * 128] = x.astype(BF16)
        return carry

    lax.fori_loop(0, 9, group, 0)


def kernel(
    feat, mask, lab, kmap, wt, cls, out, wg, cg,
    src, on, grad, hid, slope, ysend, csend, corner, rx, ry, rc, pad, pad_g, edge, band, flip, grad_t, head,
    tail, red, got, swapped, gath, send_sem, recv_sem,
):
    gx, gy = lax.axis_index("gx"), lax.axis_index("gy")
    barrier = pltpu.get_barrier_semaphore()
    peers = [(lax.rem(gx + a + NX, NX), lax.rem(gy + b + NY, NY)) for a, b in CD]
    peers += [(gx, lax.rem(gy + d, NY)) for d in range(1, NY)]
    peers += [(lax.rem(gx + d, NX), gy) for d in range(1, NX)]
    for peer in peers:
        pl.semaphore_signal(barrier, inc=1, device_id=peer, device_id_type=MESH)

    spread = one_hot((iota((16, 1024), 1) >> 6) == iota((16, 1024), 0))

    def mask_rows(i, carry):
        at = pl.multiple_of(i * 64, 64)
        wide = dot(mask[pl.ds(at, 64), :].astype(F32).astype(BF16), spread)
        on[pl.ds(at, 64), :] = wide
        s, r = i // 4, pl.multiple_of((i % 4) * 64, 64)
        src[s, pl.ds(r, 64), :] = (feat[pl.ds(at, 64), :].astype(F32) * wide).astype(BF16)
        return carry

    lax.fori_loop(0, 8, mask_rows, 0)
    fore = Halo(src, ysend.at[0], csend.at[0], corner, rx.at[0], ry.at[0], rc.at[0], send_sem, recv_sem, 0, gx, gy)
    fore.prepare()
    pl.semaphore_wait(barrier, len(peers))
    fore_copies = fore.copies()
    for copy in fore_copies:
        copy.start()

    build_bands(wt, band, flip)
    lane, row = iota((128, 1024), 1), iota((128, 1024), 0)
    repeat = one_hot((iota((64, 1024), 1) & 63) == iota((64, 1024), 0))
    kind_row = iota((128, 1), 0) >> 4
    kind_row = jnp.where(kind_row >= 6, kind_row - 6, jnp.where(kind_row >= 3, kind_row - 3, kind_row))
    wide_cls = dot(cls[...], repeat)
    diag = (lane >> 6) == (row & 15)
    classes = jnp.where(
        kind_row == 0, wide_cls[0:1], jnp.where(kind_row == 1, wide_cls[1:2], wide_cls[2:3])
    )
    head[...] = jnp.where(diag, classes, 0.0).astype(BF16)
    for copy in fore_copies:
        copy.wait_recv()

    build_padded(fore, kmap, pad, edge)

    def fore_chunk(i, carry):
        s, q = i // 4, i % 4
        pre = conv(pad, band, s, q)
        lanes = pl.ds(pl.multiple_of(q * 256, 256), 256)
        voxel = on[pl.ds(pl.multiple_of(s * 256, 256), 256), lanes]
        sig = 0.5 * jnp.tanh(0.5 * pre) + 0.5
        hid[s, :, lanes] = (pre * sig * voxel).astype(BF16)
        slope[s, :, lanes] = sig * (1.0 + pre * (1.0 - sig)) * voxel
        return carry

    lax.fori_loop(0, 8, fore_chunk, 0)

    narrow = one_hot(((iota((16, 128), 1) & 15) == iota((16, 128), 0)) & (iota((16, 128), 1) < 48))
    kind = (iota((256, 128), 1) >> 4).astype(F32)
    class_part = jnp.zeros((128, 1024), F32)
    for s in range(2):
        rows = slice(s * 256, (s + 1) * 256)
        logits = dot_t(hid[s], head[...])
        second, third = pltpu.roll(logits, 112, axis=1), pltpu.roll(logits, 96, axis=1)
        top = jnp.maximum(logits, jnp.maximum(second, third))
        mine = jnp.exp(logits - top)
        prob = mine / (mine + jnp.exp(second - top) + jnp.exp(third - top))
        voxel = dot(mask[rows, :].astype(F32).astype(BF16), narrow)
        target = dot(lab[rows, :].astype(F32).astype(BF16), narrow)
        grad_logits = ((prob - jnp.where(target == kind, 1.0, 0.0)) * voxel).astype(BF16)
        class_part += tdot(grad_logits, hid[s])
        for q in range(4):
            lanes = slice(q * 256, (q + 1) * 256)
            g = dot(grad_logits, head[:, lanes]) * slope[s, :, lanes]
            grad[s, :, lanes] = g.astype(BF16)

    back = Halo(grad, ysend.at[1], csend.at[1], corner, rx.at[1], ry.at[1], rc.at[1], send_sem, recv_sem, 8, gx, gy)
    back.prepare()
    back_copies = back.copies()
    for copy in back_copies:
        copy.start()
    for s in range(2):
        for q in range(4):
            turned = grad[s, :, q * 256 : (q + 1) * 256].astype(F32).T
            grad_t[:, (s * 4 + q) * 256 : (s * 4 + q + 1) * 256] = turned.astype(BF16)

    low = low_half(64)

    def weight_group(g, carry):
        dx, dy = g // 3, g % 3
        rows = pl.ds(pl.multiple_of(dx * 16, 16), 256)
        rhs = jnp.concatenate(
            [pad[dy, s, rows, q * 256 : q * 256 + 384] for s in range(2) for q in range(4)], axis=0
        )
        full = dot(grad_t[...], rhs)
        even = full[0:64, 0:256] + full[128:192, 128:384]
        odd = full[64:128, 0:256] + full[192:256, 128:384]
        red[g] = (even[:, :128] + swap(jnp.where(low, odd[:, 128:], odd[:, :128]))).astype(BF16)
        tail[g] = even[:, 128:] + swap(odd[:, 128:])
        return carry

    lax.fori_loop(0, 9, weight_group, 0)
    tail[9] = jnp.zeros((64, 128), F32)
    for k in range(3):
        part = jnp.where(diag[:16], class_part[k * 16 : (k + 1) * 16], 0.0)
        part = jnp.sum(part, axis=0, keepdims=True)
        total = part[:, 0:128]
        for t in range(1, 8):
            total += part[:, t * 128 : (t + 1) * 128]
        tail[9, k : k + 1, :] = total + swap(total)
    for h in range(5):
        red[9 + h] = jnp.where(low, tail[2 * h], swap(tail[2 * h + 1])).astype(BF16)
    red[14] = jnp.zeros((64, 128), BF16)
    red[15] = jnp.zeros((64, 128), BF16)

    scatter = []
    for d in range(1, NY):
        to = lax.rem(gy + d, NY)
        scatter.append(
            pltpu.make_async_remote_copy(
                src_ref=red.at[to],
                dst_ref=got.at[d],
                send_sem=send_sem.at[16 + d],
                recv_sem=recv_sem.at[16 + d],
                device_id=(gx, to),
                device_id_type=MESH,
            )
        )
    for copy in scatter:
        copy.start()

    for copy in back_copies:
        copy.wait_recv()
    build_padded(back, kmap, pad_g, edge)

    def back_chunk(i, carry):
        s, q = i // 4, i % 4
        lanes = pl.ds(pl.multiple_of(q * 256, 256), 256)
        rows = pl.ds(pl.multiple_of(s * 256, 256), 256)
        out[rows, lanes] = (conv(pad_g, flip, s, q) * on[rows, lanes]).astype(BF16)
        return carry

    lax.fori_loop(0, 4, back_chunk, 0)
    for copy in scatter:
        copy.wait_recv()
    total = red[gy].astype(F32)
    for d in range(1, NY):
        total += got[d].astype(F32)
    swapped[gx] = total.astype(BF16)
    across = []
    for d in range(1, NX):
        to = lax.rem(gx + d, NX)
        source = lax.rem(gx + NX - d, NX)
        send = pltpu.make_async_remote_copy(
            src_ref=swapped.at[gx],
            dst_ref=swapped.at[gx],
            send_sem=send_sem.at[32 + d],
            recv_sem=recv_sem.at[32 + gx],
            device_id=(to, gy),
            device_id_type=MESH,
        )
        land = pltpu.make_async_remote_copy(
            src_ref=swapped.at[gx],
            dst_ref=swapped.at[source],
            send_sem=send_sem.at[32 + d],
            recv_sem=recv_sem.at[32 + source],
            device_id=(to, gy),
            device_id_type=MESH,
        )
        send.start()
        across.append((send, land))
    lax.fori_loop(4, 8, back_chunk, 0)
    for _, land in across:
        land.wait_recv()
    total = swapped[0].astype(F32)
    for d in range(1, NX):
        total += swapped[d].astype(F32)
    gath[gy] = total.astype(BF16)
    gather = []
    for d in range(1, NY):
        to = lax.rem(gy + d, NY)
        source = lax.rem(gy + NY - d, NY)
        send = pltpu.make_async_remote_copy(
            src_ref=gath.at[gy],
            dst_ref=gath.at[gy],
            send_sem=send_sem.at[40 + d],
            recv_sem=recv_sem.at[40 + gy],
            device_id=(gx, to),
            device_id_type=MESH,
        )
        land = pltpu.make_async_remote_copy(
            src_ref=gath.at[gy],
            dst_ref=gath.at[source],
            send_sem=send_sem.at[40 + d],
            recv_sem=recv_sem.at[40 + source],
            device_id=(gx, to),
            device_id_type=MESH,
        )
        send.start()
        gather.append((send, land))
    for copy in fore_copies + back_copies + scatter + [send for send, _ in across]:
        copy.wait_send()
    for _, land in gather:
        land.wait_recv()
    scale = float(NX * NY * 2 * 16**3) ** -0.5
    for g in range(9):
        wg[g * 192 : g * 192 + 128, :] = gath[g].astype(F32).T * scale
    for h in range(5):
        turned = gath[9 + h].astype(F32).T * scale
        wg[h * 384 + 128 : h * 384 + 192, :] = turned[:64]
        if h < 4:
            wg[h * 384 + 320 : h * 384 + 384, :] = turned[64:]
    cg[...] = swap(gath[13].astype(F32) * scale)[:3, :64]
    for send, _ in gather:
        send.wait_send()


def local(features, mask, labels, kernel_map, weight, classifier):
    vmem = pl.BlockSpec(memory_space=pltpu.VMEM)
    out, wg, cg = pl.pallas_call(
        kernel,
        out_shape=(
            jax.ShapeDtypeStruct((512, 1024), BF16),
            jax.ShapeDtypeStruct((1728, 64), F32),
            jax.ShapeDtypeStruct((3, 64), F32),
        ),
        in_specs=[vmem, vmem, vmem, pl.BlockSpec(memory_space=pltpu.SMEM), vmem, vmem],
        out_specs=(vmem, vmem, vmem),
        scratch_shapes=[
            pltpu.VMEM((2, 256, 1024), BF16),
            pltpu.VMEM((512, 1024), F32),
            pltpu.VMEM((2, 256, 1024), BF16),
            pltpu.VMEM((2, 256, 1024), BF16),
            pltpu.VMEM((2, 256, 1024), F32),
            pltpu.VMEM((2, 2, 2, 16, 1024), BF16),
            pltpu.VMEM((2, 4, 16, 128), BF16),
            pltpu.VMEM((4, 16, 128), F32),
            pltpu.VMEM((2, 2, 2, 16, 1024), BF16),
            pltpu.VMEM((2, 2, 2, 16, 1024), BF16),
            pltpu.VMEM((2, 4, 16, 128), BF16),
            pltpu.VMEM((3, 2, 288, 1152), BF16),
            pltpu.VMEM((3, 2, 288, 1152), BF16),
            pltpu.VMEM((2, 2, 24, 1152), F32),
            pltpu.VMEM((3456, 256), BF16),
            pltpu.VMEM((3456, 256), BF16),
            pltpu.VMEM((256, 2048), BF16),
            pltpu.VMEM((128, 1024), BF16),
            pltpu.VMEM((10, 64, 128), F32),
            pltpu.VMEM((16, 64, 128), BF16),
            pltpu.VMEM((16, 64, 128), BF16),
            pltpu.VMEM((8, 64, 128), BF16),
            pltpu.VMEM((16, 64, 128), BF16),
            pltpu.SemaphoreType.DMA((56,)),
            pltpu.SemaphoreType.DMA((56,)),
        ],
        compiler_params=pltpu.CompilerParams(
            collective_id=0, has_side_effects=True, vmem_limit_bytes=56 * 1024 * 1024
        ),
        name="sparse_conv",
    )(
        features.reshape(512, 1024),
        mask.reshape(512, 16),
        labels.reshape(512, 16),
        kernel_map.reshape(2, 27),
        weight.reshape(1728, 64),
        classifier,
    )
    return out.reshape(1, 1, 2, 16, 16, 1024), wg.reshape(27, 64, 64), cg


def solution(mesh):
    in_specs = (
        P("gx", "gy", None, None, None, None),
        P("gx", "gy", None, None, None, None),
        P("gx", "gy", None, None, None, None),
        P("gx", "gy", None, None),
        P(),
        P(),
    )
    out_specs = (P("gx", "gy", None, None, None, None), P(), P())
    return jax.shard_map(local, mesh=mesh, in_specs=in_specs, out_specs=out_specs, check_vma=False)
```

```python
import jax
import jax.numpy as jnp
from jax import lax
from jax.experimental import pallas as pl
from jax.experimental.pallas import tpu as pltpu
from jax.sharding import PartitionSpec as P

MESH = pl.DeviceIdType.MESH
F32, BF16, I32 = jnp.float32, jnp.bfloat16, jnp.int32
NX, NY = 8, 16
CHUNKS = 14
DIRS = [(a, b) for a in (-1, 0, 1) for b in (-1, 0, 1) if (a, b) != (0, 0)]
XD = [(-1, 0), (1, 0)]
YD = [(0, -1), (0, 1)]
CD = [(-1, -1), (-1, 1), (1, -1), (1, 1)]


def iota(shape, dim):
    return lax.broadcasted_iota(I32, shape, dim)


def dot(a, b):
    return jnp.dot(a, b, preferred_element_type=F32)


def dot_t(a, b):
    return lax.dot_general(a, b, (((1,), (1,)), ((), ())), preferred_element_type=F32)


def tdot(a, b):
    return lax.dot_general(a, b, (((0,), (0,)), ((), ())), preferred_element_type=F32)


def one_hot(cond):
    return jnp.where(cond, 1.0, 0.0).astype(BF16)


def pick(m, first, second):
    return jnp.where(m == 0, first, jnp.where(m == 1, second, 0.0))


def low_half(rows):
    return iota((rows, 128), 1) < 64


def swap(x):
    return pltpu.roll(x, 64, axis=1)


def deepen(before, body, after):
    tiles = [before] + body + [after]
    low = low_half(before.shape[0])
    return [swap(jnp.where(low, tiles[k + 1], tiles[k])) for k in range(9)]


def offset_id(a, b, c):
    return (a + 1) * 9 + (b + 1) * 3 + (c + 1)


class Halo:
    def __init__(self, src, ysend, csend, corner, rx, ry, rc, send_sem, recv_sem, base, gx, gy):
        self.src, self.ysend, self.csend, self.corner = src, ysend, csend, corner
        self.rx, self.ry, self.rc = rx, ry, rc
        self.send_sem, self.recv_sem, self.base = send_sem, recv_sem, base
        self.gx, self.gy = gx, gy

    def prepare(self):
        r = iota((32, 256), 0)
        c = iota((32, 256), 1)
        sel = one_hot(c == (r & 15) * 16 + (r >> 4) * 15)
        for s in range(2):
            rows = dot(sel, self.src[s])
            self.ysend[0, s] = rows[:16].astype(BF16)
            self.ysend[1, s] = rows[16:].astype(BF16)
            for n, (a, b) in enumerate(CD):
                at = (16 if b > 0 else 0) + (15 if a > 0 else 0)
                for k in range(8):
                    self.corner[n, s * 8 + k : s * 8 + k + 1, :] = rows[at : at + 1, k * 128 : (k + 1) * 128]
        for n in range(4):
            self.csend[n] = self.corner[n].astype(BF16)

    def copies(self):
        out = []
        for n, (a, b) in enumerate(XD + YD + CD):
            if n < 2:
                src, dst, opp = self.src.at[:, pl.ds(15 * 16 if a > 0 else 0, 16), :], self.rx.at[1 - n], 1 - n
            elif n < 4:
                src, dst, opp = self.ysend.at[n - 2], self.ry.at[3 - n], 5 - n
            else:
                src, dst, opp = self.csend.at[n - 4], self.rc.at[7 - n], 11 - n
            to = (lax.rem(self.gx + a + NX, NX), lax.rem(self.gy + b + NY, NY))
            out.append(
                pltpu.make_async_remote_copy(
                    src_ref=src,
                    dst_ref=dst,
                    send_sem=self.send_sem.at[self.base + n],
                    recv_sem=self.recv_sem.at[self.base + opp],
                    device_id=to,
                    device_id_type=MESH,
                )
            )
        return out


def split_tiles(x):
    return [x[:, k * 128 : (k + 1) * 128] for k in range(x.shape[1] // 128)]


def spread_planes(tiles, low_row, high_row):
    rows = iota((16, 128), 0)
    down, up = [], []
    for k, t in enumerate(tiles):
        lanes = slice(k * 128, (k + 1) * 128)
        first = 0.0 if low_row is None else low_row[:, lanes]
        last = 0.0 if high_row is None else high_row[:, lanes]
        down.append(jnp.where(rows == 0, first, pltpu.roll(t, 1, axis=0)))
        up.append(jnp.where(rows == 15, last, pltpu.roll(t, 15, axis=0)))
    return down, tiles, up


def put(pad, s, plane, tiles, low_row=None, high_row=None):
    at = pl.multiple_of(plane * 16, 16)
    for dy, version in enumerate(spread_planes(tiles, low_row, high_row)):
        for k, t in enumerate(version):
            pad[dy, s, pl.ds(at, 16), k * 128 : (k + 1) * 128] = t.astype(BF16)


def from_slots(kmap, s, a, b, one, two):
    m = [kmap[s, offset_id(a, b, c)] for c in (-1, 0, 1)]
    return deepen(
        pick(m[0], one[:, 896:], two[:, 896:]),
        split_tiles(pick(m[1], one, two)),
        pick(m[2], one[:, :128], two[:, :128]),
    )


def own_tiles(src, kmap, s, x):
    rows = pl.ds(pl.multiple_of(x * 16, 16), 16)
    before = pick(kmap[s, 12], src[0, rows, 896:1024].astype(F32), src[1, rows, 896:1024].astype(F32))
    after = pick(kmap[s, 14], src[0, rows, 0:128].astype(F32), src[1, rows, 0:128].astype(F32))
    return deepen(before, split_tiles(src[s, rows, :].astype(F32)), after)


def corner_rows(halo, kmap, edge):
    low = low_half(8)
    for n, (a, b) in enumerate(CD):
        packed = halo.rc[n].astype(F32)
        e, w = (b + 1) // 2, (a + 1) // 2
        for s in range(2):
            m = [kmap[s, offset_id(a, b, c)] for c in (-1, 0, 1)]
            before, mid, after = (pick(v, packed[:8], packed[8:]) for v in m)
            prev = pltpu.roll(jnp.where(iota((8, 128), 0) == 7, before, mid), 1, axis=0)
            body = swap(jnp.where(low, mid, prev))
            last = swap(jnp.where(low, pltpu.roll(after, 7, axis=0), mid))
            for k in range(8):
                edge[e, s, 16 + w : 17 + w, k * 128 : (k + 1) * 128] = body[k : k + 1]
            edge[e, s, 16 + w : 17 + w, 1024:1152] = last[7:8]


def build_local(src, kmap, pad):
    for s in range(2):
        for dy in range(3):
            pad[dy, s, 0:16, :] = jnp.zeros((16, 1152), BF16)
            pad[dy, s, 272:288, :] = jnp.zeros((16, 1152), BF16)

        def plane(x, carry):
            put(pad, s, x + 1, own_tiles(src, kmap, s, x))
            return carry

        lax.fori_loop(0, 16, plane, 0, unroll=4)


def build_sides(halo, kmap, side, edge):
    corner_rows(halo, kmap, edge)
    for s in range(2):
        for w, (a, _) in enumerate(XD):
            tiles = from_slots(kmap, s, a, 0, halo.rx[w, 0].astype(F32), halo.rx[w, 1].astype(F32))
            versions = spread_planes(tiles, edge[0, s, 16 + w : 17 + w, :], edge[1, s, 16 + w : 17 + w, :])
            put_side(side, w, s, versions)
        for e, (_, b) in enumerate(YD):
            tiles = from_slots(kmap, s, 0, b, halo.ry[e, 0].astype(F32), halo.ry[e, 1].astype(F32))
            put_side(side, 2 + e, s, spread_planes(tiles, None, None))


def put_side(side, n, s, versions):
    for shift, tiles in enumerate(versions):
        cast = [t.astype(BF16) for t in tiles]
        for q in range(4):
            for k in range(3):
                at = (s * 4 + q) * 16
                lanes = shift * 384 + k * 128
                side[n, at : at + 16, lanes : lanes + 128] = cast[2 * q + k]


def add_sides(side, band, acc, beyond):
    for n in range(4):
        end = n % 2
        if n < 2:
            part = dot(side[n], band[end * 2304 : end * 2304 + 1152, :])
        else:
            at = [(dx * 3 + 2 * end) * 384 for dx in range(3)]
            part = dot(side[n], jnp.concatenate([band[i : i + 384, :] for i in at], axis=0))
        for s in range(2):
            for q in range(4):
                lanes = slice(q * 256, (q + 1) * 256)
                term = part[(s * 4 + q) * 16 : (s * 4 + q) * 16 + 16]
                if n < 2:
                    acc[s, 240 * end : 240 * end + 16, lanes] += term
                else:
                    beyond[end, s, :, lanes] = term


def build_padded(halo, kmap, pad, edge):
    corner_rows(halo, kmap, edge)
    for s in range(2):
        for e, (_, b) in enumerate(YD):
            tiles = from_slots(kmap, s, 0, b, halo.ry[e, 0].astype(F32), halo.ry[e, 1].astype(F32))
            edge[e, s, 0:16, :] = jnp.concatenate(tiles, axis=1)
        for w, (a, _) in enumerate(XD):
            tiles = from_slots(kmap, s, a, 0, halo.rx[w, 0].astype(F32), halo.rx[w, 1].astype(F32))
            put(pad, s, 17 * w, tiles, edge[0, s, 16 + w : 17 + w, :], edge[1, s, 16 + w : 17 + w, :])

        def plane(x, carry):
            put(pad, s, x + 1, own_tiles(halo.src, kmap, s, x), edge[0, s, pl.ds(x, 1), :], edge[1, s, pl.ds(x, 1), :])
            return carry

        lax.fori_loop(0, 16, plane, 0, unroll=4)


def conv(pad, band, q):
    lanes = pl.ds(pl.multiple_of(q * 256, 256), 384)
    pieces = [
        jnp.concatenate([pad[dy, s, pl.ds(dx * 16, 256), lanes] for s in range(2)], axis=0)
        for dx in range(3)
        for dy in range(3)
    ]
    return dot(jnp.concatenate(pieces, axis=1), band[...])


def build_bands(wt, band, flip):
    dup = one_hot((iota((64, 128), 1) & 63) == iota((64, 128), 0))
    low = low_half(64)
    zero = jnp.zeros((64, 128), F32)

    def group(g, carry):
        fore = dot(wt[pl.ds(pl.multiple_of(g * 192, 64), 192), :], dup)
        parts = [fore[d * 64 : (d + 1) * 64] for d in range(3)]
        back = [tdot(wt[pl.ds(pl.multiple_of((8 - g) * 192 + (2 - d) * 64, 64), 64), :], dup) for d in range(3)]
        for which, ref in ((parts, band), (back, flip)):
            for i in range(6):
                for t in range(2):
                    a, b = i - 2 * t, i - 2 * t - 1
                    x = jnp.where(low, which[a] if 0 <= a < 3 else zero, which[b] if 0 <= b < 3 else zero)
                    at = pl.multiple_of(g * 384 + i * 64, 64)
                    ref[pl.ds(at, 64), t * 128 : (t + 1) * 128] = x.astype(BF16)
        return carry

    lax.fori_loop(0, 9, group, 0)


def kernel(
    feat_h, mask_h, lab_h, kmap, wt_h, cls, out_h, gath_h,
    feat, mask, lab, wt, out, src, on, grad, hid, slope, ysend, csend, corner, rx, ry, rc, pad, pad_g, edge, side, beyond,
    band, flip, grad_t, head, tail, red, got, swapped, gath, local_sem, send_sem, recv_sem,
):
    gx, gy = lax.axis_index("gx"), lax.axis_index("gy")
    half = [pl.ds(0, 256), pl.ds(256, 256)]
    loads = [
        pltpu.make_async_copy(a, b, local_sem.at[n])
        for n, (a, b) in enumerate(
            [(mask_h, mask)] + [(feat_h.at[h, :], feat.at[h, :]) for h in half] + [(wt_h, wt), (lab_h, lab)]
        )
    ]
    for load in loads:
        load.start()
    barrier = pltpu.get_barrier_semaphore()
    peers = [(lax.rem(gx + a + NX, NX), lax.rem(gy + b + NY, NY)) for a, b in CD]
    peers += [(gx, lax.rem(gy + d, NY)) for d in range(1, NY)]
    peers += [(lax.rem(gx + d, NX), gy) for d in range(1, NX)]
    for peer in peers:
        pl.semaphore_signal(barrier, inc=1, device_id=peer, device_id_type=MESH)

    spread = one_hot((iota((16, 1024), 1) >> 6) == iota((16, 1024), 0))

    def mask_rows(i, carry):
        at = pl.multiple_of(i * 64, 64)
        wide = dot(mask[pl.ds(at, 64), :].astype(F32).astype(BF16), spread)
        on[pl.ds(at, 64), :] = wide
        s, r = i // 4, pl.multiple_of((i % 4) * 64, 64)
        src[s, pl.ds(r, 64), :] = (feat[pl.ds(at, 64), :].astype(F32) * wide).astype(BF16)
        return carry

    loads[0].wait()
    loads[1].wait()
    loads[2].wait()
    lax.fori_loop(0, 8, mask_rows, 0)
    fore = Halo(src, ysend.at[0], csend.at[0], corner, rx.at[0], ry.at[0], rc.at[0], send_sem, recv_sem, 0, gx, gy)
    fore.prepare()
    pl.semaphore_wait(barrier, len(peers))
    fore_copies = fore.copies()
    for copy in fore_copies:
        copy.start()

    loads[3].wait()
    loads[4].wait()
    build_bands(wt, band, flip)
    lane, row = iota((128, 1024), 1), iota((128, 1024), 0)
    repeat = one_hot((iota((64, 1024), 1) & 63) == iota((64, 1024), 0))
    kind_row = iota((128, 1), 0) >> 4
    kind_row = jnp.where(kind_row >= 6, kind_row - 6, jnp.where(kind_row >= 3, kind_row - 3, kind_row))
    wide_cls = dot(cls[...], repeat)
    diag = (lane >> 6) == (row & 15)
    classes = jnp.where(
        kind_row == 0, wide_cls[0:1], jnp.where(kind_row == 1, wide_cls[1:2], wide_cls[2:3])
    )
    head[...] = jnp.where(diag, classes, 0.0).astype(BF16)
    build_local(src, kmap, pad)

    def fore_chunk(q, carry):
        pre = conv(pad, band, q)
        lanes = pl.ds(pl.multiple_of(q * 256, 256), 256)
        for s in range(2):
            slope[s, :, lanes] = pre[s * 256 : (s + 1) * 256]
        return carry

    lax.fori_loop(0, 4, fore_chunk, 0)

    for copy in fore_copies:
        copy.wait_recv()
    build_sides(fore, kmap, side, edge)
    add_sides(side, band, slope, beyond)

    def activate(i, carry):
        s, x = i // 16, i % 16
        rows = pl.ds(pl.multiple_of(x * 16, 16), 16)
        y = iota((16, 1024), 0)
        pre = slope[s, rows, :] + jnp.where(y == 0, beyond[0, s, pl.ds(x, 1), :], 0.0)
        pre = pre + jnp.where(y == 15, beyond[1, s, pl.ds(x, 1), :], 0.0)
        voxel = on[pl.ds(pl.multiple_of(i * 16, 16), 16), :]
        sig = 0.5 * jnp.tanh(0.5 * pre) + 0.5
        hid[s, rows, :] = (pre * sig * voxel).astype(BF16)
        slope[s, rows, :] = sig * (1.0 + pre * (1.0 - sig)) * voxel
        return carry

    lax.fori_loop(0, 32, activate, 0, unroll=2)
    narrow = one_hot(((iota((16, 128), 1) & 15) == iota((16, 128), 0)) & (iota((16, 128), 1) < 48))
    kind = (iota((256, 128), 1) >> 4).astype(F32)
    class_part = jnp.zeros((128, 1024), F32)
    for s in range(2):
        rows = slice(s * 256, (s + 1) * 256)
        logits = dot_t(hid[s], head[...])
        second, third = pltpu.roll(logits, 112, axis=1), pltpu.roll(logits, 96, axis=1)
        top = jnp.maximum(logits, jnp.maximum(second, third))
        mine = jnp.exp(logits - top)
        prob = mine / (mine + jnp.exp(second - top) + jnp.exp(third - top))
        voxel = dot(mask[rows, :].astype(F32).astype(BF16), narrow)
        target = dot(lab[rows, :].astype(F32).astype(BF16), narrow)
        grad_logits = ((prob - jnp.where(target == kind, 1.0, 0.0)) * voxel).astype(BF16)
        class_part += tdot(grad_logits, hid[s])
        for q in range(4):
            lanes = slice(q * 256, (q + 1) * 256)
            g = dot(grad_logits, head[:, lanes]) * slope[s, :, lanes]
            grad[s, :, lanes] = g.astype(BF16)

    back = Halo(grad, ysend.at[1], csend.at[1], corner, rx.at[1], ry.at[1], rc.at[1], send_sem, recv_sem, 8, gx, gy)
    back.prepare()
    back_copies = back.copies()
    for copy in back_copies:
        copy.start()
    for s in range(2):
        for q in range(4):
            turned = grad[s, :, q * 256 : (q + 1) * 256].astype(F32).T
            grad_t[:, (s * 4 + q) * 256 : (s * 4 + q + 1) * 256] = turned.astype(BF16)
    for n in range(4):
        rows = []
        for s in range(2):
            plane = grad[s, 240 * n : 240 * n + 16, :] if n < 2 else back.ysend[n - 2, s]
            rows += [plane[:, q * 256 : (q + 1) * 256] for q in range(4)]
        turned = jnp.concatenate(rows, axis=0).astype(F32).T
        grad_t[:, 2048 + n * 128 : 2176 + n * 128] = turned.astype(BF16)

    low = low_half(64)
    none = jnp.zeros((128, 384), BF16)
    for dx in range(3):
        rows = pl.ds(dx * 16, 256)
        lhs, rhs = [grad_t[:, 0:2048]], []
        for s in range(2):
            for q in range(4):
                rhs.append(jnp.concatenate([pad[dy, s, rows, q * 256 : q * 256 + 384] for dy in range(3)], axis=1))
        over = slice(dx * 384, (dx + 1) * 384)
        lhs.append(grad_t[:, 2304:2560])
        rhs.append(jnp.concatenate([side[2, :, over], none, none], axis=1))
        rhs.append(jnp.concatenate([none, none, side[3, :, over]], axis=1))
        if dx != 1:
            w = dx // 2
            lhs.append(grad_t[:, 2048 + w * 128 : 2176 + w * 128])
            rhs.append(side[w])
        wide = dot(jnp.concatenate(lhs, axis=1), jnp.concatenate(rhs, axis=0))
        for dy in range(3):
            full = wide[:, dy * 384 : (dy + 1) * 384]
            even = full[0:64, 0:256] + full[128:192, 128:384]
            odd = full[64:128, 0:256] + full[192:256, 128:384]
            red[dx * 3 + dy] = (even[:, :128] + swap(jnp.where(low, odd[:, 128:], odd[:, :128]))).astype(BF16)
            tail[dx * 3 + dy] = even[:, 128:] + swap(odd[:, 128:])
    tail[9] = jnp.zeros((64, 128), F32)
    for k in range(3):
        part = jnp.where(diag[:16], class_part[k * 16 : (k + 1) * 16], 0.0)
        part = jnp.sum(part, axis=0, keepdims=True)
        total = part[:, 0:128]
        for t in range(1, 8):
            total += part[:, t * 128 : (t + 1) * 128]
        tail[9, k : k + 1, :] = total + swap(total)
    for h in range(5):
        red[9 + h] = jnp.where(low, tail[2 * h], swap(tail[2 * h + 1])).astype(BF16)
    red[14] = jnp.zeros((64, 128), BF16)
    red[15] = jnp.zeros((64, 128), BF16)

    scatter = []
    for d in range(1, NY):
        to = lax.rem(gy + d, NY)
        scatter.append(
            pltpu.make_async_remote_copy(
                src_ref=red.at[to],
                dst_ref=got.at[d],
                send_sem=send_sem.at[16 + d],
                recv_sem=recv_sem.at[16 + d],
                device_id=(gx, to),
                device_id_type=MESH,
            )
        )
    for copy in scatter:
        copy.start()

    for copy in back_copies:
        copy.wait_recv()
    build_padded(back, kmap, pad_g, edge)

    for copy in scatter:
        copy.wait_recv()
    total = red[gy].astype(F32)
    for d in range(1, NY):
        total += got[d].astype(F32)
    swapped[gx] = total.astype(BF16)
    across = share(swapped, gx, NX, lambda to: (to, gy), send_sem, recv_sem, 32)
    for send, _ in across:
        send.start()

    def back_chunk(q, carry):
        lanes = pl.ds(pl.multiple_of(q * 256, 256), 256)
        out[:, lanes] = (conv(pad_g, flip, q) * on[:, lanes]).astype(BF16)
        return carry

    stores = [
        pltpu.make_async_copy(out.at[:, pl.ds(i * 512, 512)], out_h.at[:, pl.ds(i * 512, 512)], local_sem.at[5 + i])
        for i in range(2)
    ]
    lax.fori_loop(0, 2, back_chunk, 0)
    stores[0].start()
    for _, land in across:
        land.wait_recv()
    total = swapped[0].astype(F32)
    for d in range(1, NX):
        total += swapped[d].astype(F32)
    gath[gy] = total.astype(BF16)
    gather = share(gath, gy, NY, lambda to: (gx, to), send_sem, recv_sem, 40)
    for send, _ in gather:
        send.start()
    lax.fori_loop(2, 4, back_chunk, 0)
    stores[1].start()
    for copy in fore_copies + back_copies + scatter + [send for send, _ in across]:
        copy.wait_send()
    for _, land in gather:
        land.wait_recv()
    stores.append(pltpu.make_async_copy(gath, gath_h, local_sem.at[7]))
    stores[2].start()
    for send, _ in gather:
        send.wait_send()
    for store in stores:
        store.wait()


def share(ref, me, count, device, send_sem, recv_sem, base):
    pairs = []
    for d in range(1, count):
        to, source = lax.rem(me + d, count), lax.rem(me + count - d, count)
        pairs.append(
            [
                pltpu.make_async_remote_copy(
                    src_ref=ref.at[me],
                    dst_ref=ref.at[entry],
                    send_sem=send_sem.at[base + d],
                    recv_sem=recv_sem.at[base + entry],
                    device_id=device(to),
                    device_id_type=MESH,
                )
                for entry in (me, source)
            ]
        )
    return pairs


def finish(out_h, gath, grad_h, wg, cg, buf, sem):
    parts = [pl.ds(i * 128, 128) for i in range(4)]
    loads = [pltpu.make_async_copy(out_h.at[p, :], buf.at[p, :], sem.at[i]) for i, p in enumerate(parts)]
    stores = [pltpu.make_async_copy(buf.at[p, :], grad_h.at[p, :], sem.at[4 + i]) for i, p in enumerate(parts)]
    for load in loads:
        load.start()
    for load, store in zip(loads, stores):
        load.wait()
        store.start()
    scale = float(NX * NY * 2 * 16**3) ** -0.5
    for g in range(9):
        wg[g * 192 : g * 192 + 128, :] = gath[g].astype(F32).T * scale
    for h in range(5):
        turned = gath[9 + h].astype(F32).T * scale
        wg[h * 384 + 128 : h * 384 + 192, :] = turned[:64]
        if h < 4:
            wg[h * 384 + 320 : h * 384 + 384, :] = turned[64:]
    cg[...] = swap(gath[13].astype(F32) * scale)[:3, :64]
    for store in stores:
        store.wait()


def local(features, mask, labels, kernel_map, weight, classifier):
    vmem, anywhere = pl.BlockSpec(memory_space=pltpu.VMEM), pl.BlockSpec(memory_space=pl.ANY)
    out, gath = pl.pallas_call(
        kernel,
        out_shape=(jax.ShapeDtypeStruct((512, 1024), BF16), jax.ShapeDtypeStruct((16, 64, 128), BF16)),
        in_specs=[anywhere, anywhere, anywhere, pl.BlockSpec(memory_space=pltpu.SMEM), anywhere, vmem],
        out_specs=(anywhere, anywhere),
        scratch_shapes=[
            pltpu.VMEM((512, 1024), BF16),
            pltpu.VMEM((512, 16), I32),
            pltpu.VMEM((512, 16), I32),
            pltpu.VMEM((1728, 64), BF16),
            pltpu.VMEM((512, 1024), BF16),
            pltpu.VMEM((2, 256, 1024), BF16),
            pltpu.VMEM((512, 1024), F32),
            pltpu.VMEM((2, 256, 1024), BF16),
            pltpu.VMEM((2, 256, 1024), BF16),
            pltpu.VMEM((2, 256, 1024), F32),
            pltpu.VMEM((2, 2, 2, 16, 1024), BF16),
            pltpu.VMEM((2, 4, 16, 128), BF16),
            pltpu.VMEM((4, 16, 128), F32),
            pltpu.VMEM((2, 2, 2, 16, 1024), BF16),
            pltpu.VMEM((2, 2, 2, 16, 1024), BF16),
            pltpu.VMEM((2, 4, 16, 128), BF16),
            pltpu.VMEM((3, 2, 288, 1152), BF16),
            pltpu.VMEM((3, 2, 288, 1152), BF16),
            pltpu.VMEM((2, 2, 24, 1152), F32),
            pltpu.VMEM((4, 128, 1152), BF16),
            pltpu.VMEM((2, 2, 16, 1024), F32),
            pltpu.VMEM((3456, 256), BF16),
            pltpu.VMEM((3456, 256), BF16),
            pltpu.VMEM((256, 2560), BF16),
            pltpu.VMEM((128, 1024), BF16),
            pltpu.VMEM((10, 64, 128), F32),
            pltpu.VMEM((16, 64, 128), BF16),
            pltpu.VMEM((16, 64, 128), BF16),
            pltpu.VMEM((8, 64, 128), BF16),
            pltpu.VMEM((16, 64, 128), BF16),
            pltpu.SemaphoreType.DMA((8,)),
            pltpu.SemaphoreType.DMA((56,)),
            pltpu.SemaphoreType.DMA((56,)),
        ],
        compiler_params=pltpu.CompilerParams(
            collective_id=0, has_side_effects=True, vmem_limit_bytes=56 * 1024 * 1024
        ),
        name="sparse_conv",
    )(
        features.reshape(512, 1024),
        mask.reshape(512, 16),
        labels.reshape(512, 16),
        kernel_map.reshape(2, 27),
        weight.reshape(1728, 64),
        classifier,
    )
    grad_input, wg, cg = pl.pallas_call(
        finish,
        out_shape=(
            jax.ShapeDtypeStruct((512, 1024), BF16),
            jax.ShapeDtypeStruct((1728, 64), F32),
            jax.ShapeDtypeStruct((3, 64), F32),
        ),
        in_specs=[anywhere, vmem],
        out_specs=(anywhere, vmem, vmem),
        scratch_shapes=[pltpu.VMEM((512, 1024), BF16), pltpu.SemaphoreType.DMA((8,))],
        name="finish",
    )(out, gath)
    return grad_input.reshape(1, 1, 2, 16, 16, 1024), wg.reshape(27, 64, 64), cg


def solution(mesh):
    in_specs = (
        P("gx", "gy", None, None, None, None),
        P("gx", "gy", None, None, None, None),
        P("gx", "gy", None, None, None, None),
        P("gx", "gy", None, None),
        P(),
        P(),
    )
    out_specs = (P("gx", "gy", None, None, None, None), P(), P())
    return jax.shard_map(local, mesh=mesh, in_specs=in_specs, out_specs=out_specs, check_vma=False)
```

```python
import jax
import jax.numpy as jnp
from jax import lax
from jax.experimental import pallas as pl
from jax.experimental.pallas import tpu as pltpu
from jax.sharding import PartitionSpec as P

MESH = pl.DeviceIdType.MESH
F32, BF16, I32 = jnp.float32, jnp.bfloat16, jnp.int32
NX, NY = 8, 16
CHUNKS = 14
DIRS = [(a, b) for a in (-1, 0, 1) for b in (-1, 0, 1) if (a, b) != (0, 0)]
XD = [(-1, 0), (1, 0)]
YD = [(0, -1), (0, 1)]
CD = [(-1, -1), (-1, 1), (1, -1), (1, 1)]


def iota(shape, dim):
    return lax.broadcasted_iota(I32, shape, dim)


def dot(a, b):
    return jnp.dot(a, b, preferred_element_type=F32)


def dot_t(a, b):
    return lax.dot_general(a, b, (((1,), (1,)), ((), ())), preferred_element_type=F32)


def tdot(a, b):
    return lax.dot_general(a, b, (((0,), (0,)), ((), ())), preferred_element_type=F32)


def one_hot(cond):
    return jnp.where(cond, 1.0, 0.0).astype(BF16)


def pick(m, first, second):
    return jnp.where(m == 0, first, jnp.where(m == 1, second, 0.0))


def low_half(rows):
    return iota((rows, 128), 1) < 64


def swap(x):
    return pltpu.roll(x, 64, axis=1)


def deepen(before, body, after):
    tiles = [before] + body + [after]
    low = low_half(before.shape[0])
    return [swap(jnp.where(low, tiles[k + 1], tiles[k])) for k in range(9)]


def offset_id(a, b, c):
    return (a + 1) * 9 + (b + 1) * 3 + (c + 1)


class Halo:
    def __init__(self, src, ysend, csend, corner, rx, ry, rc, send_sem, recv_sem, base, gx, gy):
        self.src, self.ysend, self.csend, self.corner = src, ysend, csend, corner
        self.rx, self.ry, self.rc = rx, ry, rc
        self.send_sem, self.recv_sem, self.base = send_sem, recv_sem, base
        self.gx, self.gy = gx, gy

    def prepare(self):
        r = iota((32, 256), 0)
        c = iota((32, 256), 1)
        sel = one_hot(c == (r & 15) * 16 + (r >> 4) * 15)
        for s in range(2):
            rows = dot(sel, self.src[s])
            self.ysend[0, s] = rows[:16].astype(BF16)
            self.ysend[1, s] = rows[16:].astype(BF16)
            for n, (a, b) in enumerate(CD):
                at = (16 if b > 0 else 0) + (15 if a > 0 else 0)
                for k in range(8):
                    self.corner[n, s * 8 + k : s * 8 + k + 1, :] = rows[at : at + 1, k * 128 : (k + 1) * 128]
        for n in range(4):
            self.csend[n] = self.corner[n].astype(BF16)

    def copies(self):
        out = []
        for n, (a, b) in enumerate(XD + YD + CD):
            if n < 2:
                src, dst, opp = self.src.at[:, pl.ds(15 * 16 if a > 0 else 0, 16), :], self.rx.at[1 - n], 1 - n
            elif n < 4:
                src, dst, opp = self.ysend.at[n - 2], self.ry.at[3 - n], 5 - n
            else:
                src, dst, opp = self.csend.at[n - 4], self.rc.at[7 - n], 11 - n
            to = (lax.rem(self.gx + a + NX, NX), lax.rem(self.gy + b + NY, NY))
            out.append(
                pltpu.make_async_remote_copy(
                    src_ref=src,
                    dst_ref=dst,
                    send_sem=self.send_sem.at[self.base + n],
                    recv_sem=self.recv_sem.at[self.base + opp],
                    device_id=to,
                    device_id_type=MESH,
                )
            )
        return out


def split_tiles(x):
    return [x[:, k * 128 : (k + 1) * 128] for k in range(x.shape[1] // 128)]


def spread_planes(tiles, low_row, high_row):
    rows = iota((16, 128), 0)
    down, up = [], []
    for k, t in enumerate(tiles):
        lanes = slice(k * 128, (k + 1) * 128)
        first = 0.0 if low_row is None else low_row[:, lanes]
        last = 0.0 if high_row is None else high_row[:, lanes]
        down.append(jnp.where(rows == 0, first, pltpu.roll(t, 1, axis=0)))
        up.append(jnp.where(rows == 15, last, pltpu.roll(t, 15, axis=0)))
    return down, tiles, up


def put(pad, s, plane, tiles, low_row=None, high_row=None):
    at = pl.multiple_of(plane * 16, 16)
    for dy, version in enumerate(spread_planes(tiles, low_row, high_row)):
        for k, t in enumerate(version):
            pad[dy, s, pl.ds(at, 16), k * 128 : (k + 1) * 128] = t.astype(BF16)


def from_slots(kmap, s, a, b, one, two):
    m = [kmap[s, offset_id(a, b, c)] for c in (-1, 0, 1)]
    return deepen(
        pick(m[0], one[:, 896:], two[:, 896:]),
        split_tiles(pick(m[1], one, two)),
        pick(m[2], one[:, :128], two[:, :128]),
    )


def own_tiles(src, kmap, s, x):
    rows = pl.ds(pl.multiple_of(x * 16, 16), 16)
    before = pick(kmap[s, 12], src[0, rows, 896:1024].astype(F32), src[1, rows, 896:1024].astype(F32))
    after = pick(kmap[s, 14], src[0, rows, 0:128].astype(F32), src[1, rows, 0:128].astype(F32))
    return deepen(before, split_tiles(src[s, rows, :].astype(F32)), after)


def corner_rows(halo, kmap, edge):
    low = low_half(8)
    for n, (a, b) in enumerate(CD):
        packed = halo.rc[n].astype(F32)
        e, w = (b + 1) // 2, (a + 1) // 2
        for s in range(2):
            m = [kmap[s, offset_id(a, b, c)] for c in (-1, 0, 1)]
            before, mid, after = (pick(v, packed[:8], packed[8:]) for v in m)
            prev = pltpu.roll(jnp.where(iota((8, 128), 0) == 7, before, mid), 1, axis=0)
            body = swap(jnp.where(low, mid, prev))
            last = swap(jnp.where(low, pltpu.roll(after, 7, axis=0), mid))
            for k in range(8):
                edge[e, s, 16 + w : 17 + w, k * 128 : (k + 1) * 128] = body[k : k + 1]
            edge[e, s, 16 + w : 17 + w, 1024:1152] = last[7:8]


def build_local(src, kmap, pad):
    for s in range(2):
        for dy in range(3):
            pad[dy, s, 0:16, :] = jnp.zeros((16, 1152), BF16)
            pad[dy, s, 272:288, :] = jnp.zeros((16, 1152), BF16)

        def plane(x, carry):
            put(pad, s, x + 1, own_tiles(src, kmap, s, x))
            return carry

        lax.fori_loop(0, 16, plane, 0, unroll=4)


def build_sides(halo, kmap, side, edge):
    corner_rows(halo, kmap, edge)
    for s in range(2):
        for w, (a, _) in enumerate(XD):
            tiles = from_slots(kmap, s, a, 0, halo.rx[w, 0].astype(F32), halo.rx[w, 1].astype(F32))
            versions = spread_planes(tiles, edge[0, s, 16 + w : 17 + w, :], edge[1, s, 16 + w : 17 + w, :])
            put_side(side, w, s, versions)
        for e, (_, b) in enumerate(YD):
            tiles = from_slots(kmap, s, 0, b, halo.ry[e, 0].astype(F32), halo.ry[e, 1].astype(F32))
            put_side(side, 2 + e, s, spread_planes(tiles, None, None))


def put_side(side, n, s, versions):
    for shift, tiles in enumerate(versions):
        cast = [t.astype(BF16) for t in tiles]
        for q in range(4):
            for k in range(3):
                at = (s * 4 + q) * 16
                lanes = shift * 384 + k * 128
                side[n, at : at + 16, lanes : lanes + 128] = cast[2 * q + k]


def add_sides(side, band, acc, beyond):
    for n in range(4):
        end = n % 2
        if n < 2:
            part = dot(side[n], band[end * 2304 : end * 2304 + 1152, :])
        else:
            at = [(dx * 3 + 2 * end) * 384 for dx in range(3)]
            part = dot(side[n], jnp.concatenate([band[i : i + 384, :] for i in at], axis=0))
        for s in range(2):
            for q in range(4):
                lanes = slice(q * 256, (q + 1) * 256)
                term = part[(s * 4 + q) * 16 : (s * 4 + q) * 16 + 16]
                if n < 2:
                    acc[s, 240 * end : 240 * end + 16, lanes] += term
                else:
                    beyond[end, s, :, lanes] = term


def build_padded(halo, kmap, pad, edge):
    corner_rows(halo, kmap, edge)
    for s in range(2):
        for e, (_, b) in enumerate(YD):
            tiles = from_slots(kmap, s, 0, b, halo.ry[e, 0].astype(F32), halo.ry[e, 1].astype(F32))
            edge[e, s, 0:16, :] = jnp.concatenate(tiles, axis=1)
        for w, (a, _) in enumerate(XD):
            tiles = from_slots(kmap, s, a, 0, halo.rx[w, 0].astype(F32), halo.rx[w, 1].astype(F32))
            put(pad, s, 17 * w, tiles, edge[0, s, 16 + w : 17 + w, :], edge[1, s, 16 + w : 17 + w, :])

        def plane(x, carry):
            put(pad, s, x + 1, own_tiles(halo.src, kmap, s, x), edge[0, s, pl.ds(x, 1), :], edge[1, s, pl.ds(x, 1), :])
            return carry

        lax.fori_loop(0, 16, plane, 0, unroll=4)


def conv(pad, band, q):
    lanes = pl.ds(pl.multiple_of(q * 256, 256), 384)
    pieces = [
        jnp.concatenate([pad[dy, s, pl.ds(dx * 16, 256), lanes] for s in range(2)], axis=0)
        for dx in range(3)
        for dy in range(3)
    ]
    return dot(jnp.concatenate(pieces, axis=1), band[...])


def build_bands(wt, band, flip):
    dup = one_hot((iota((64, 128), 1) & 63) == iota((64, 128), 0))
    low = low_half(64)
    zero = jnp.zeros((64, 128), F32)

    def group(g, carry):
        fore = dot(wt[pl.ds(pl.multiple_of(g * 192, 64), 192), :], dup)
        parts = [fore[d * 64 : (d + 1) * 64] for d in range(3)]
        back = [tdot(wt[pl.ds(pl.multiple_of((8 - g) * 192 + (2 - d) * 64, 64), 64), :], dup) for d in range(3)]
        for which, ref in ((parts, band), (back, flip)):
            for i in range(6):
                for t in range(2):
                    a, b = i - 2 * t, i - 2 * t - 1
                    x = jnp.where(low, which[a] if 0 <= a < 3 else zero, which[b] if 0 <= b < 3 else zero)
                    at = pl.multiple_of(g * 384 + i * 64, 64)
                    ref[pl.ds(at, 64), t * 128 : (t + 1) * 128] = x.astype(BF16)
        return carry

    lax.fori_loop(0, 9, group, 0)


def kernel(
    feat_h, mask_h, lab_h, kmap_h, wt_h, cls_h, out, wg, cg,
    feat, mask, lab, kmap, wt, cls, src, on, grad, hid, slope, ysend, csend, corner, rx, ry, rc, pad, pad_g, edge, side, beyond,
    band, flip, grad_t, head, tail, red, got, swapped, gath, local_sem, send_sem, recv_sem,
):
    gx, gy = lax.axis_index("gx"), lax.axis_index("gy")
    half = [pl.ds(0, 256), pl.ds(256, 256)]
    loads = [
        pltpu.make_async_copy(a, b, local_sem.at[n])
        for n, (a, b) in enumerate(
            [(mask_h, mask)] + [(feat_h.at[h, :], feat.at[h, :]) for h in half] + [(kmap_h, kmap), (wt_h, wt), (cls_h, cls), (lab_h, lab)]
        )
    ]
    for load in loads:
        load.start()
    barrier = pltpu.get_barrier_semaphore()
    peers = [(lax.rem(gx + a + NX, NX), lax.rem(gy + b + NY, NY)) for a, b in CD]
    peers += [(gx, lax.rem(gy + d, NY)) for d in range(1, NY)]
    peers += [(lax.rem(gx + d, NX), gy) for d in range(1, NX)]
    for peer in peers:
        pl.semaphore_signal(barrier, inc=1, device_id=peer, device_id_type=MESH)

    spread = one_hot((iota((16, 1024), 1) >> 6) == iota((16, 1024), 0))

    def mask_rows(i, carry):
        at = pl.multiple_of(i * 64, 64)
        wide = dot(mask[pl.ds(at, 64), :].astype(F32).astype(BF16), spread)
        on[pl.ds(at, 64), :] = wide
        s, r = i // 4, pl.multiple_of((i % 4) * 64, 64)
        src[s, pl.ds(r, 64), :] = (feat[pl.ds(at, 64), :].astype(F32) * wide).astype(BF16)
        return carry

    loads[0].wait()
    loads[1].wait()
    loads[2].wait()
    lax.fori_loop(0, 8, mask_rows, 0)
    fore = Halo(src, ysend.at[0], csend.at[0], corner, rx.at[0], ry.at[0], rc.at[0], send_sem, recv_sem, 0, gx, gy)
    fore.prepare()
    pl.semaphore_wait(barrier, len(peers))
    fore_copies = fore.copies()
    for copy in fore_copies:
        copy.start()

    for load in loads[3:]:
        load.wait()
    build_bands(wt, band, flip)
    lane, row = iota((128, 1024), 1), iota((128, 1024), 0)
    repeat = one_hot((iota((64, 1024), 1) & 63) == iota((64, 1024), 0))
    kind_row = iota((128, 1), 0) >> 4
    kind_row = jnp.where(kind_row >= 6, kind_row - 6, jnp.where(kind_row >= 3, kind_row - 3, kind_row))
    wide_cls = dot(cls[...], repeat)
    diag = (lane >> 6) == (row & 15)
    classes = jnp.where(
        kind_row == 0, wide_cls[0:1], jnp.where(kind_row == 1, wide_cls[1:2], wide_cls[2:3])
    )
    head[...] = jnp.where(diag, classes, 0.0).astype(BF16)
    build_local(src, kmap, pad)

    def fore_chunk(q, carry):
        pre = conv(pad, band, q)
        lanes = pl.ds(pl.multiple_of(q * 256, 256), 256)
        for s in range(2):
            slope[s, :, lanes] = pre[s * 256 : (s + 1) * 256]
        return carry

    lax.fori_loop(0, 4, fore_chunk, 0)

    for copy in fore_copies:
        copy.wait_recv()
    build_sides(fore, kmap, side, edge)
    add_sides(side, band, slope, beyond)

    def activate(i, carry):
        s, x = i // 16, i % 16
        rows = pl.ds(pl.multiple_of(x * 16, 16), 16)
        y = iota((16, 1024), 0)
        pre = slope[s, rows, :] + jnp.where(y == 0, beyond[0, s, pl.ds(x, 1), :], 0.0)
        pre = pre + jnp.where(y == 15, beyond[1, s, pl.ds(x, 1), :], 0.0)
        voxel = on[pl.ds(pl.multiple_of(i * 16, 16), 16), :]
        sig = 0.5 * jnp.tanh(0.5 * pre) + 0.5
        hid[s, rows, :] = (pre * sig * voxel).astype(BF16)
        slope[s, rows, :] = sig * (1.0 + pre * (1.0 - sig)) * voxel
        return carry

    lax.fori_loop(0, 32, activate, 0, unroll=2)
    narrow = one_hot(((iota((16, 128), 1) & 15) == iota((16, 128), 0)) & (iota((16, 128), 1) < 48))
    kind = (iota((256, 128), 1) >> 4).astype(F32)
    class_part = jnp.zeros((128, 1024), F32)
    for s in range(2):
        rows = slice(s * 256, (s + 1) * 256)
        logits = dot_t(hid[s], head[...])
        second, third = pltpu.roll(logits, 112, axis=1), pltpu.roll(logits, 96, axis=1)
        top = jnp.maximum(logits, jnp.maximum(second, third))
        mine = jnp.exp(logits - top)
        prob = mine / (mine + jnp.exp(second - top) + jnp.exp(third - top))
        voxel = dot(mask[rows, :].astype(F32).astype(BF16), narrow)
        target = dot(lab[rows, :].astype(F32).astype(BF16), narrow)
        grad_logits = ((prob - jnp.where(target == kind, 1.0, 0.0)) * voxel).astype(BF16)
        class_part += tdot(grad_logits, hid[s])
        for q in range(4):
            lanes = slice(q * 256, (q + 1) * 256)
            g = dot(grad_logits, head[:, lanes]) * slope[s, :, lanes]
            grad[s, :, lanes] = g.astype(BF16)

    back = Halo(grad, ysend.at[1], csend.at[1], corner, rx.at[1], ry.at[1], rc.at[1], send_sem, recv_sem, 8, gx, gy)
    back.prepare()
    back_copies = back.copies()
    for copy in back_copies:
        copy.start()
    for s in range(2):
        for q in range(4):
            turned = grad[s, :, q * 256 : (q + 1) * 256].astype(F32).T
            grad_t[:, (s * 4 + q) * 256 : (s * 4 + q + 1) * 256] = turned.astype(BF16)
    for n in range(4):
        rows = []
        for s in range(2):
            plane = grad[s, 240 * n : 240 * n + 16, :] if n < 2 else back.ysend[n - 2, s]
            rows += [plane[:, q * 256 : (q + 1) * 256] for q in range(4)]
        turned = jnp.concatenate(rows, axis=0).astype(F32).T
        grad_t[:, 2048 + n * 128 : 2176 + n * 128] = turned.astype(BF16)

    low = low_half(64)
    none = jnp.zeros((128, 384), BF16)
    for dx in range(3):
        rows = pl.ds(dx * 16, 256)
        lhs, rhs = [grad_t[:, 0:2048]], []
        for s in range(2):
            for q in range(4):
                rhs.append(jnp.concatenate([pad[dy, s, rows, q * 256 : q * 256 + 384] for dy in range(3)], axis=1))
        over = slice(dx * 384, (dx + 1) * 384)
        lhs.append(grad_t[:, 2304:2560])
        rhs.append(jnp.concatenate([side[2, :, over], none, none], axis=1))
        rhs.append(jnp.concatenate([none, none, side[3, :, over]], axis=1))
        if dx != 1:
            w = dx // 2
            lhs.append(grad_t[:, 2048 + w * 128 : 2176 + w * 128])
            rhs.append(side[w])
        wide = dot(jnp.concatenate(lhs, axis=1), jnp.concatenate(rhs, axis=0))
        for dy in range(3):
            full = wide[:, dy * 384 : (dy + 1) * 384]
            even = full[0:64, 0:256] + full[128:192, 128:384]
            odd = full[64:128, 0:256] + full[192:256, 128:384]
            red[dx * 3 + dy] = (even[:, :128] + swap(jnp.where(low, odd[:, 128:], odd[:, :128]))).astype(BF16)
            tail[dx * 3 + dy] = even[:, 128:] + swap(odd[:, 128:])
    tail[9] = jnp.zeros((64, 128), F32)
    for k in range(3):
        part = jnp.where(diag[:16], class_part[k * 16 : (k + 1) * 16], 0.0)
        part = jnp.sum(part, axis=0, keepdims=True)
        total = part[:, 0:128]
        for t in range(1, 8):
            total += part[:, t * 128 : (t + 1) * 128]
        tail[9, k : k + 1, :] = total + swap(total)
    for h in range(5):
        red[9 + h] = jnp.where(low, tail[2 * h], swap(tail[2 * h + 1])).astype(BF16)
    red[14] = jnp.zeros((64, 128), BF16)
    red[15] = jnp.zeros((64, 128), BF16)

    scatter = []
    for d in range(1, NY):
        to = lax.rem(gy + d, NY)
        scatter.append(
            pltpu.make_async_remote_copy(
                src_ref=red.at[to],
                dst_ref=got.at[d],
                send_sem=send_sem.at[16 + d],
                recv_sem=recv_sem.at[16 + d],
                device_id=(gx, to),
                device_id_type=MESH,
            )
        )
    for copy in scatter:
        copy.start()

    for copy in back_copies:
        copy.wait_recv()
    build_padded(back, kmap, pad_g, edge)

    for copy in scatter:
        copy.wait_recv()
    total = red[gy].astype(F32)
    for d in range(1, NY):
        total += got[d].astype(F32)
    swapped[gx] = total.astype(BF16)
    across = share(swapped, gx, NX, lambda to: (to, gy), send_sem, recv_sem, 32)
    for send, _ in across:
        send.start()

    def back_chunk(q, carry):
        lanes = pl.ds(pl.multiple_of(q * 256, 256), 256)
        out[:, lanes] = (conv(pad_g, flip, q) * on[:, lanes]).astype(BF16)
        return carry

    lax.fori_loop(0, 2, back_chunk, 0)
    for _, land in across:
        land.wait_recv()
    total = swapped[0].astype(F32)
    for d in range(1, NX):
        total += swapped[d].astype(F32)
    gath[gy] = total.astype(BF16)
    gather = share(gath, gy, NY, lambda to: (gx, to), send_sem, recv_sem, 40)
    for send, _ in gather:
        send.start()
    lax.fori_loop(2, 4, back_chunk, 0)
    for copy in fore_copies + back_copies + scatter + [send for send, _ in across]:
        copy.wait_send()
    for _, land in gather:
        land.wait_recv()
    scale = float(NX * NY * 2 * 16**3) ** -0.5
    for g in range(9):
        wg[g * 192 : g * 192 + 128, :] = gath[g].astype(F32).T * scale
    for h in range(5):
        turned = gath[9 + h].astype(F32).T * scale
        wg[h * 384 + 128 : h * 384 + 192, :] = turned[:64]
        if h < 4:
            wg[h * 384 + 320 : h * 384 + 384, :] = turned[64:]
    cg[...] = swap(gath[13].astype(F32) * scale)[:3, :64]
    for send, _ in gather:
        send.wait_send()


def share(ref, me, count, device, send_sem, recv_sem, base):
    pairs = []
    for d in range(1, count):
        to, source = lax.rem(me + d, count), lax.rem(me + count - d, count)
        pairs.append(
            [
                pltpu.make_async_remote_copy(
                    src_ref=ref.at[me],
                    dst_ref=ref.at[entry],
                    send_sem=send_sem.at[base + d],
                    recv_sem=recv_sem.at[base + entry],
                    device_id=device(to),
                    device_id_type=MESH,
                )
                for entry in (me, source)
            ]
        )
    return pairs


def finish(*refs):
    sources, results, sem = refs[:3], refs[3:6], refs[6]
    copies = [pltpu.make_async_copy(sources[i], results[i], sem.at[i]) for i in range(3)]
    for copy in copies:
        copy.start()
    for copy in copies:
        copy.wait()


def local(features, mask, labels, kernel_map, weight, classifier):
    vmem, anywhere = pl.BlockSpec(memory_space=pltpu.VMEM), pl.BlockSpec(memory_space=pl.ANY)
    shapes = [((512, 1024), BF16), ((1728, 64), F32), ((3, 64), F32)]
    results = pl.pallas_call(
        kernel,
        out_shape=[pltpu.VMEM(*shape) for shape in shapes],
        in_specs=[anywhere] * 6,
        out_specs=[vmem] * 3,
        scratch_shapes=[
            pltpu.VMEM((512, 1024), BF16),
            pltpu.VMEM((512, 16), I32),
            pltpu.VMEM((512, 16), I32),
            pltpu.SMEM((2, 27), I32),
            pltpu.VMEM((1728, 64), BF16),
            pltpu.VMEM((3, 64), BF16),
            pltpu.VMEM((2, 256, 1024), BF16),
            pltpu.VMEM((512, 1024), F32),
            pltpu.VMEM((2, 256, 1024), BF16),
            pltpu.VMEM((2, 256, 1024), BF16),
            pltpu.VMEM((2, 256, 1024), F32),
            pltpu.VMEM((2, 2, 2, 16, 1024), BF16),
            pltpu.VMEM((2, 4, 16, 128), BF16),
            pltpu.VMEM((4, 16, 128), F32),
            pltpu.VMEM((2, 2, 2, 16, 1024), BF16),
            pltpu.VMEM((2, 2, 2, 16, 1024), BF16),
            pltpu.VMEM((2, 4, 16, 128), BF16),
            pltpu.VMEM((3, 2, 288, 1152), BF16),
            pltpu.VMEM((3, 2, 288, 1152), BF16),
            pltpu.VMEM((2, 2, 24, 1152), F32),
            pltpu.VMEM((4, 128, 1152), BF16),
            pltpu.VMEM((2, 2, 16, 1024), F32),
            pltpu.VMEM((3456, 256), BF16),
            pltpu.VMEM((3456, 256), BF16),
            pltpu.VMEM((256, 2560), BF16),
            pltpu.VMEM((128, 1024), BF16),
            pltpu.VMEM((10, 64, 128), F32),
            pltpu.VMEM((16, 64, 128), BF16),
            pltpu.VMEM((16, 64, 128), BF16),
            pltpu.VMEM((8, 64, 128), BF16),
            pltpu.VMEM((16, 64, 128), BF16),
            pltpu.SemaphoreType.DMA((7,)),
            pltpu.SemaphoreType.DMA((56,)),
            pltpu.SemaphoreType.DMA((56,)),
        ],
        compiler_params=pltpu.CompilerParams(
            collective_id=0, has_side_effects=True, vmem_limit_bytes=40 * 1024 * 1024
        ),
        name="sparse_conv",
    )(
        *[
            pltpu.with_memory_space_constraint(x, pltpu.HBM)
            for x in (
                features.reshape(512, 1024),
                mask.reshape(512, 16),
                labels.reshape(512, 16),
                kernel_map.reshape(2, 27),
                weight.reshape(1728, 64),
                classifier,
            )
        ]
    )
    grad_input, wg, cg = pl.pallas_call(
        finish,
        out_shape=[pltpu.HBM(*shape) for shape in shapes],
        in_specs=[vmem] * 3,
        out_specs=[anywhere] * 3,
        scratch_shapes=[pltpu.SemaphoreType.DMA((3,))],
        name="finish",
    )(*[pltpu.with_memory_space_constraint(x, pltpu.VMEM) for x in results])
    return grad_input.reshape(1, 1, 2, 16, 16, 1024), wg.reshape(27, 64, 64), cg


def solution(mesh):
    in_specs = (
        P("gx", "gy", None, None, None, None),
        P("gx", "gy", None, None, None, None),
        P("gx", "gy", None, None, None, None),
        P("gx", "gy", None, None),
        P(),
        P(),
    )
    out_specs = (P("gx", "gy", None, None, None, None), P(), P())
    return jax.shard_map(local, mesh=mesh, in_specs=in_specs, out_specs=out_specs, check_vma=False)
```

```python
import jax
import jax.numpy as jnp
from jax import lax
from jax.experimental import pallas as pl
from jax.experimental.pallas import tpu as pltpu
from jax.sharding import PartitionSpec as P

MESH = pl.DeviceIdType.MESH
F32, BF16, I32 = jnp.float32, jnp.bfloat16, jnp.int32
NX, NY = 8, 16
CHUNKS = 14
OWNER = [t * 5 % NY for t in range(CHUNKS)]
PARTS = [(0, 4), (4, 9), (9, 14)]
WHOLE = [0, 1, 2, 4, 5, 6, 9, 10, 11]
PAIRS = [3, 7, 8, 12, 13]
DIRS = [(a, b) for a in (-1, 0, 1) for b in (-1, 0, 1) if (a, b) != (0, 0)]
XD = [(-1, 0), (1, 0)]
YD = [(0, -1), (0, 1)]
CD = [(-1, -1), (-1, 1), (1, -1), (1, 1)]


def iota(shape, dim):
    return lax.broadcasted_iota(I32, shape, dim)


def dot(a, b):
    return jnp.dot(a, b, preferred_element_type=F32)


def dot_t(a, b):
    return lax.dot_general(a, b, (((1,), (1,)), ((), ())), preferred_element_type=F32)


def tdot(a, b):
    return lax.dot_general(a, b, (((0,), (0,)), ((), ())), preferred_element_type=F32)


def one_hot(cond):
    return jnp.where(cond, 1.0, 0.0).astype(BF16)


def pick(m, first, second):
    return jnp.where(m == 0, first, jnp.where(m == 1, second, 0.0))


def low_half(rows):
    return iota((rows, 128), 1) < 64


def swap(x):
    return pltpu.roll(x, 64, axis=1)


def deepen(before, body, after):
    tiles = [before] + body + [after]
    low = low_half(before.shape[0])
    return [swap(jnp.where(low, tiles[k + 1], tiles[k])) for k in range(9)]


def offset_id(a, b, c):
    return (a + 1) * 9 + (b + 1) * 3 + (c + 1)


class Halo:
    def __init__(self, src, ysend, csend, corner, rx, ry, rc, send_sem, recv_sem, base, gx, gy):
        self.src, self.ysend, self.csend, self.corner = src, ysend, csend, corner
        self.rx, self.ry, self.rc = rx, ry, rc
        self.send_sem, self.recv_sem, self.base = send_sem, recv_sem, base
        self.gx, self.gy = gx, gy

    def prepare(self):
        r = iota((32, 256), 0)
        c = iota((32, 256), 1)
        sel = one_hot(c == (r & 15) * 16 + (r >> 4) * 15)
        for s in range(2):
            rows = dot(sel, self.src[s])
            self.ysend[0, s] = rows[:16].astype(BF16)
            self.ysend[1, s] = rows[16:].astype(BF16)
            for n, (a, b) in enumerate(CD):
                at = (16 if b > 0 else 0) + (15 if a > 0 else 0)
                for k in range(8):
                    self.corner[n, s * 8 + k : s * 8 + k + 1, :] = rows[at : at + 1, k * 128 : (k + 1) * 128]
        for n in range(4):
            self.csend[n] = self.corner[n].astype(BF16)

    def copies(self):
        out = []
        for n, (a, b) in enumerate(XD + YD + CD):
            if n < 2:
                src, dst, opp = self.src.at[:, pl.ds(15 * 16 if a > 0 else 0, 16), :], self.rx.at[1 - n], 1 - n
            elif n < 4:
                src, dst, opp = self.ysend.at[n - 2], self.ry.at[3 - n], 5 - n
            else:
                src, dst, opp = self.csend.at[n - 4], self.rc.at[7 - n], 11 - n
            to = (lax.rem(self.gx + a + NX, NX), lax.rem(self.gy + b + NY, NY))
            out.append(
                pltpu.make_async_remote_copy(
                    src_ref=src,
                    dst_ref=dst,
                    send_sem=self.send_sem.at[self.base + n],
                    recv_sem=self.recv_sem.at[self.base + opp],
                    device_id=to,
                    device_id_type=MESH,
                )
            )
        return out


def split_tiles(x):
    return [x[:, k * 128 : (k + 1) * 128] for k in range(x.shape[1] // 128)]


def spread_planes(tiles, low_row, high_row):
    rows = iota((16, 128), 0)
    down, up = [], []
    for k, t in enumerate(tiles):
        lanes = slice(k * 128, (k + 1) * 128)
        first = 0.0 if low_row is None else low_row[:, lanes]
        last = 0.0 if high_row is None else high_row[:, lanes]
        down.append(jnp.where(rows == 0, first, pltpu.roll(t, 1, axis=0)))
        up.append(jnp.where(rows == 15, last, pltpu.roll(t, 15, axis=0)))
    return down, tiles, up


def put(pad, s, plane, tiles, low_row=None, high_row=None):
    at = pl.multiple_of(plane * 16, 16)
    for dy, version in enumerate(spread_planes(tiles, low_row, high_row)):
        for k, t in enumerate(version):
            pad[dy, s, pl.ds(at, 16), k * 128 : (k + 1) * 128] = t.astype(BF16)


def from_slots(kmap, s, a, b, one, two):
    m = [kmap[s, offset_id(a, b, c)] for c in (-1, 0, 1)]
    return deepen(
        pick(m[0], one[:, 896:], two[:, 896:]),
        split_tiles(pick(m[1], one, two)),
        pick(m[2], one[:, :128], two[:, :128]),
    )


def own_tiles(src, kmap, s, x):
    rows = pl.ds(pl.multiple_of(x * 16, 16), 16)
    before = pick(kmap[s, 12], src[0, rows, 896:1024].astype(F32), src[1, rows, 896:1024].astype(F32))
    after = pick(kmap[s, 14], src[0, rows, 0:128].astype(F32), src[1, rows, 0:128].astype(F32))
    return deepen(before, split_tiles(src[s, rows, :].astype(F32)), after)


def corner_rows(halo, kmap, edge):
    low = low_half(8)
    for n, (a, b) in enumerate(CD):
        packed = halo.rc[n].astype(F32)
        e, w = (b + 1) // 2, (a + 1) // 2
        for s in range(2):
            m = [kmap[s, offset_id(a, b, c)] for c in (-1, 0, 1)]
            before, mid, after = (pick(v, packed[:8], packed[8:]) for v in m)
            prev = pltpu.roll(jnp.where(iota((8, 128), 0) == 7, before, mid), 1, axis=0)
            body = swap(jnp.where(low, mid, prev))
            last = swap(jnp.where(low, pltpu.roll(after, 7, axis=0), mid))
            for k in range(8):
                edge[e, s, 16 + w : 17 + w, k * 128 : (k + 1) * 128] = body[k : k + 1]
            edge[e, s, 16 + w : 17 + w, 1024:1152] = last[7:8]


def build_local(src, kmap, pad):
    for s in range(2):
        for dy in range(3):
            pad[dy, s, 0:16, :] = jnp.zeros((16, 1152), BF16)
            pad[dy, s, 272:288, :] = jnp.zeros((16, 1152), BF16)

        def plane(x, carry):
            put(pad, s, x + 1, own_tiles(src, kmap, s, x))
            return carry

        lax.fori_loop(0, 16, plane, 0, unroll=4)


def build_sides(halo, kmap, side, edge):
    corner_rows(halo, kmap, edge)
    for s in range(2):
        for w, (a, _) in enumerate(XD):
            tiles = from_slots(kmap, s, a, 0, halo.rx[w, 0].astype(F32), halo.rx[w, 1].astype(F32))
            versions = spread_planes(tiles, edge[0, s, 16 + w : 17 + w, :], edge[1, s, 16 + w : 17 + w, :])
            put_side(side, w, s, versions)
        for e, (_, b) in enumerate(YD):
            tiles = from_slots(kmap, s, 0, b, halo.ry[e, 0].astype(F32), halo.ry[e, 1].astype(F32))
            put_side(side, 2 + e, s, spread_planes(tiles, None, None))


def put_side(side, n, s, versions):
    for shift, tiles in enumerate(versions):
        cast = [t.astype(BF16) for t in tiles]
        for q in range(4):
            for k in range(3):
                at = (s * 4 + q) * 16
                lanes = shift * 384 + k * 128
                side[n, at : at + 16, lanes : lanes + 128] = cast[2 * q + k]


def add_sides(side, band, acc, beyond):
    for n in range(4):
        end = n % 2
        if n < 2:
            part = dot(side[n], band[end * 2304 : end * 2304 + 1152, :])
        else:
            at = [(dx * 3 + 2 * end) * 384 for dx in range(3)]
            part = dot(side[n], jnp.concatenate([band[i : i + 384, :] for i in at], axis=0))
        for s in range(2):
            for q in range(4):
                lanes = slice(q * 256, (q + 1) * 256)
                term = part[(s * 4 + q) * 16 : (s * 4 + q) * 16 + 16]
                if n < 2:
                    acc[s, 240 * end : 240 * end + 16, lanes] += term
                else:
                    beyond[end, s, :, lanes] = term


def build_padded(halo, kmap, pad, edge):
    corner_rows(halo, kmap, edge)
    for s in range(2):
        for e, (_, b) in enumerate(YD):
            tiles = from_slots(kmap, s, 0, b, halo.ry[e, 0].astype(F32), halo.ry[e, 1].astype(F32))
            edge[e, s, 0:16, :] = jnp.concatenate(tiles, axis=1)
        for w, (a, _) in enumerate(XD):
            tiles = from_slots(kmap, s, a, 0, halo.rx[w, 0].astype(F32), halo.rx[w, 1].astype(F32))
            put(pad, s, 17 * w, tiles, edge[0, s, 16 + w : 17 + w, :], edge[1, s, 16 + w : 17 + w, :])

        def plane(x, carry):
            put(pad, s, x + 1, own_tiles(halo.src, kmap, s, x), edge[0, s, pl.ds(x, 1), :], edge[1, s, pl.ds(x, 1), :])
            return carry

        lax.fori_loop(0, 16, plane, 0, unroll=4)


def conv(pad, band, q):
    lanes = pl.ds(pl.multiple_of(q * 256, 256), 384)
    pieces = [
        jnp.concatenate([pad[dy, s, pl.ds(dx * 16, 256), lanes] for s in range(2)], axis=0)
        for dx in range(3)
        for dy in range(3)
    ]
    return dot(jnp.concatenate(pieces, axis=1), band[...])


def build_bands(wt, band, flip):
    dup = one_hot((iota((64, 128), 1) & 63) == iota((64, 128), 0))
    low = low_half(64)
    zero = jnp.zeros((64, 128), F32)

    def group(g, carry):
        fore = dot(wt[pl.ds(pl.multiple_of(g * 192, 64), 192), :], dup)
        parts = [fore[d * 64 : (d + 1) * 64] for d in range(3)]
        back = [tdot(wt[pl.ds(pl.multiple_of((8 - g) * 192 + (2 - d) * 64, 64), 64), :], dup) for d in range(3)]
        for which, ref in ((parts, band), (back, flip)):
            for i in range(6):
                for t in range(2):
                    a, b = i - 2 * t, i - 2 * t - 1
                    x = jnp.where(low, which[a] if 0 <= a < 3 else zero, which[b] if 0 <= b < 3 else zero)
                    at = pl.multiple_of(g * 384 + i * 64, 64)
                    ref[pl.ds(at, 64), t * 128 : (t + 1) * 128] = x.astype(BF16)
        return carry

    lax.fori_loop(0, 9, group, 0)


class Reduction:
    def __init__(self, gx, gy, mine, red, got, swapped, gath, send_sem, recv_sem):
        self.gx, self.gy, self.mine = gx, gy, mine
        self.red, self.got, self.swapped, self.gath = red, got, swapped, gath
        self.send_sem, self.recv_sem = send_sem, recv_sem

    def copy(self, src, dst, send, recv, device):
        return pltpu.make_async_remote_copy(
            src_ref=src,
            dst_ref=dst,
            send_sem=self.send_sem.at[send],
            recv_sem=self.recv_sem.at[recv],
            device_id=device,
            device_id_type=MESH,
        )

    def to_owner(self, t, source):
        return self.copy(self.red.at[t], self.got.at[source], 16 + t, 16 + source, (self.gx, OWNER[t]))

    def to_owners_beside(self, d, source):
        to = (lax.rem(self.gx + d, NX), self.gy)
        return self.copy(self.swapped.at[self.gx], self.swapped.at[source], 32 + d, 32 + source, to)

    def to_all(self, d, t):
        to = (self.gx, lax.rem(self.gy + d, NY))
        return self.copy(self.gath.at[t], self.gath.at[t], 40 + d, 40 + t, to)

    def owns(self, part):
        return (self.mine >= PARTS[part][0]) & (self.mine < PARTS[part][1])

    def scatter(self, part):
        for t in range(*PARTS[part]):

            @pl.when(self.gy != OWNER[t])
            def _():
                self.to_owner(t, self.gy).start()

    def across(self, part):
        @pl.when(self.owns(part))
        def _():
            total = self.red[self.mine].astype(F32)
            for d in range(1, NY):
                source = lax.rem(self.gy + d, NY)
                self.to_owner(0, source).wait_recv()
                total += self.got[source].astype(F32)
            self.swapped[self.gx] = total.astype(BF16)
            for d in range(1, NX):
                self.to_owners_beside(d, self.gx).start()

    def gather(self, part):
        @pl.when(self.owns(part))
        def _():
            for d in range(1, NX):
                self.to_owners_beside(d, lax.rem(self.gx + NX - d, NX)).wait_recv()
            total = self.swapped[0].astype(F32)
            for d in range(1, NX):
                total += self.swapped[d].astype(F32)
            self.gath[self.mine] = total.astype(BF16)
            for d in range(1, NY):
                self.to_all(d, self.mine).start()

    def wait_sums(self):
        for t in range(CHUNKS):

            @pl.when(self.gy != OWNER[t])
            def _():
                self.to_owner(t, self.gy).wait_send()
                self.to_all(1, t).wait_recv()

    def wait_sent(self):
        @pl.when(self.mine < CHUNKS)
        def _():
            for d in range(1, NX):
                self.to_owners_beside(d, self.gx).wait_send()
            for d in range(1, NY):
                self.to_all(d, self.mine).wait_send()


def kernel(
    feat_h, mask_h, lab_h, kmap_h, wt_h, cls_h, out, wg, cg,
    feat, mask, lab, kmap, wt, cls, src, on, grad, hid, slope, ysend, csend, corner, rx, ry, rc, pad, pad_g, edge, side, beyond,
    band, flip, grad_t, head, tail, red, got, swapped, gath, local_sem, send_sem, recv_sem,
):
    gx, gy = lax.axis_index("gx"), lax.axis_index("gy")
    half = [pl.ds(0, 256), pl.ds(256, 256)]
    loads = [
        pltpu.make_async_copy(a, b, local_sem.at[n])
        for n, (a, b) in enumerate(
            [(mask_h, mask)] + [(feat_h.at[h, :], feat.at[h, :]) for h in half] + [(kmap_h, kmap), (wt_h, wt), (cls_h, cls), (lab_h, lab)]
        )
    ]
    for load in loads:
        load.start()
    barrier = pltpu.get_barrier_semaphore()
    peers = [(lax.rem(gx + a + NX, NX), lax.rem(gy + b + NY, NY)) for a, b in CD]
    peers += [(gx, lax.rem(gy + d, NY)) for d in range(1, NY)]
    peers += [(lax.rem(gx + d, NX), gy) for d in range(1, NX)]
    for peer in peers:
        pl.semaphore_signal(barrier, inc=1, device_id=peer, device_id_type=MESH)

    spread = one_hot((iota((16, 1024), 1) >> 6) == iota((16, 1024), 0))

    def mask_rows(i, carry):
        at = pl.multiple_of(i * 64, 64)
        wide = dot(mask[pl.ds(at, 64), :].astype(F32).astype(BF16), spread)
        on[pl.ds(at, 64), :] = wide
        s, r = i // 4, pl.multiple_of((i % 4) * 64, 64)
        src[s, pl.ds(r, 64), :] = (feat[pl.ds(at, 64), :].astype(F32) * wide).astype(BF16)
        return carry

    loads[0].wait()
    loads[1].wait()
    loads[2].wait()
    lax.fori_loop(0, 8, mask_rows, 0)
    fore = Halo(src, ysend.at[0], csend.at[0], corner, rx.at[0], ry.at[0], rc.at[0], send_sem, recv_sem, 0, gx, gy)
    fore.prepare()
    pl.semaphore_wait(barrier, len(peers))
    fore_copies = fore.copies()
    for copy in fore_copies:
        copy.start()

    for load in loads[3:]:
        load.wait()
    build_bands(wt, band, flip)
    lane, row = iota((128, 1024), 1), iota((128, 1024), 0)
    repeat = one_hot((iota((64, 1024), 1) & 63) == iota((64, 1024), 0))
    kind_row = iota((128, 1), 0) >> 4
    kind_row = jnp.where(kind_row >= 6, kind_row - 6, jnp.where(kind_row >= 3, kind_row - 3, kind_row))
    wide_cls = dot(cls[...], repeat)
    diag = (lane >> 6) == (row & 15)
    classes = jnp.where(
        kind_row == 0, wide_cls[0:1], jnp.where(kind_row == 1, wide_cls[1:2], wide_cls[2:3])
    )
    head[...] = jnp.where(diag, classes, 0.0).astype(BF16)
    build_local(src, kmap, pad)

    def fore_chunk(q, carry):
        pre = conv(pad, band, q)
        lanes = pl.ds(pl.multiple_of(q * 256, 256), 256)
        for s in range(2):
            slope[s, :, lanes] = pre[s * 256 : (s + 1) * 256]
        return carry

    lax.fori_loop(0, 4, fore_chunk, 0)

    for copy in fore_copies:
        copy.wait_recv()
    build_sides(fore, kmap, side, edge)
    add_sides(side, band, slope, beyond)

    def activate(i, carry):
        s, x = i // 16, i % 16
        rows = pl.ds(pl.multiple_of(x * 16, 16), 16)
        y = iota((16, 1024), 0)
        pre = slope[s, rows, :] + jnp.where(y == 0, beyond[0, s, pl.ds(x, 1), :], 0.0)
        pre = pre + jnp.where(y == 15, beyond[1, s, pl.ds(x, 1), :], 0.0)
        voxel = on[pl.ds(pl.multiple_of(i * 16, 16), 16), :]
        sig = 0.5 * jnp.tanh(0.5 * pre) + 0.5
        hid[s, rows, :] = (pre * sig * voxel).astype(BF16)
        slope[s, rows, :] = sig * (1.0 + pre * (1.0 - sig)) * voxel
        return carry

    lax.fori_loop(0, 32, activate, 0, unroll=2)
    narrow = one_hot(((iota((16, 128), 1) & 15) == iota((16, 128), 0)) & (iota((16, 128), 1) < 48))
    kind = (iota((256, 128), 1) >> 4).astype(F32)
    class_part = jnp.zeros((128, 1024), F32)
    for s in range(2):
        rows = slice(s * 256, (s + 1) * 256)
        logits = dot_t(hid[s], head[...])
        second, third = pltpu.roll(logits, 112, axis=1), pltpu.roll(logits, 96, axis=1)
        top = jnp.maximum(logits, jnp.maximum(second, third))
        mine = jnp.exp(logits - top)
        prob = mine / (mine + jnp.exp(second - top) + jnp.exp(third - top))
        voxel = dot(mask[rows, :].astype(F32).astype(BF16), narrow)
        target = dot(lab[rows, :].astype(F32).astype(BF16), narrow)
        grad_logits = ((prob - jnp.where(target == kind, 1.0, 0.0)) * voxel).astype(BF16)
        class_part += tdot(grad_logits, hid[s])
        for q in range(4):
            lanes = slice(q * 256, (q + 1) * 256)
            g = dot(grad_logits, head[:, lanes]) * slope[s, :, lanes]
            grad[s, :, lanes] = g.astype(BF16)

    back = Halo(grad, ysend.at[1], csend.at[1], corner, rx.at[1], ry.at[1], rc.at[1], send_sem, recv_sem, 8, gx, gy)
    back.prepare()
    back_copies = back.copies()
    for copy in back_copies:
        copy.start()
    for s in range(2):
        for q in range(4):
            turned = grad[s, :, q * 256 : (q + 1) * 256].astype(F32).T
            grad_t[:, (s * 4 + q) * 256 : (s * 4 + q + 1) * 256] = turned.astype(BF16)
    for n in range(4):
        rows = []
        for s in range(2):
            plane = grad[s, 240 * n : 240 * n + 16, :] if n < 2 else back.ysend[n - 2, s]
            rows += [plane[:, q * 256 : (q + 1) * 256] for q in range(4)]
        turned = jnp.concatenate(rows, axis=0).astype(F32).T
        grad_t[:, 2048 + n * 128 : 2176 + n * 128] = turned.astype(BF16)

    low = low_half(64)
    none = jnp.zeros((128, 384), BF16)
    mine = lax.rem(gy * 13, NY)
    reduction = Reduction(gx, gy, mine, red, got, swapped, gath, send_sem, recv_sem)
    for k in range(3):
        part = jnp.where(diag[:16], class_part[k * 16 : (k + 1) * 16], 0.0)
        part = jnp.sum(part, axis=0, keepdims=True)
        total = part[:, 0:128]
        for t in range(1, 8):
            total += part[:, t * 128 : (t + 1) * 128]
        tail[9, k : k + 1, :] = total + swap(total)
    tail[9, 3:64, :] = jnp.zeros((61, 128), F32)
    for dx in range(3):
        rows = pl.ds(dx * 16, 256)
        lhs, rhs = [grad_t[:, 0:2048]], []
        for s in range(2):
            for q in range(4):
                rhs.append(jnp.concatenate([pad[dy, s, rows, q * 256 : q * 256 + 384] for dy in range(3)], axis=1))
        over = slice(dx * 384, (dx + 1) * 384)
        lhs.append(grad_t[:, 2304:2560])
        rhs.append(jnp.concatenate([side[2, :, over], none, none], axis=1))
        rhs.append(jnp.concatenate([none, none, side[3, :, over]], axis=1))
        if dx != 1:
            w = dx // 2
            lhs.append(grad_t[:, 2048 + w * 128 : 2176 + w * 128])
            rhs.append(side[w])
        wide = dot(jnp.concatenate(lhs, axis=1), jnp.concatenate(rhs, axis=0))
        for dy in range(3):
            full = wide[:, dy * 384 : (dy + 1) * 384]
            even = full[0:64, 0:256] + full[128:192, 128:384]
            odd = full[64:128, 0:256] + full[192:256, 128:384]
            whole = even[:, :128] + swap(jnp.where(low, odd[:, 128:], odd[:, :128]))
            red[WHOLE[dx * 3 + dy]] = whole.astype(BF16)
            tail[dx * 3 + dy] = even[:, 128:] + swap(odd[:, 128:])
        for h in ((0,), (1, 2), (3, 4))[dx]:
            red[PAIRS[h]] = jnp.where(low, tail[2 * h], swap(tail[2 * h + 1])).astype(BF16)
        reduction.scatter(dx)
    reduction.across(0)

    for copy in back_copies:
        copy.wait_recv()
    build_padded(back, kmap, pad_g, edge)

    reduction.across(1)

    def back_chunk(q, carry):
        lanes = pl.ds(pl.multiple_of(q * 256, 256), 256)
        out[:, lanes] = (conv(pad_g, flip, q) * on[:, lanes]).astype(BF16)
        return carry

    lax.fori_loop(0, 2, back_chunk, 0)
    reduction.across(2)
    reduction.gather(0)
    lax.fori_loop(2, 4, back_chunk, 0)
    reduction.gather(1)
    reduction.gather(2)
    for copy in fore_copies + back_copies:
        copy.wait_send()
    reduction.wait_sums()
    scale = float(NX * NY * 2 * 16**3) ** -0.5
    for g in range(9):
        wg[g * 192 : g * 192 + 128, :] = gath[WHOLE[g]].astype(F32).T * scale
    for h in range(5):
        turned = gath[PAIRS[h]].astype(F32).T * scale
        wg[h * 384 + 128 : h * 384 + 192, :] = turned[:64]
        if h < 4:
            wg[h * 384 + 320 : h * 384 + 384, :] = turned[64:]
    cg[...] = swap(gath[13].astype(F32) * scale)[:3, :64]
    reduction.wait_sent()


def finish(*refs):
    sources, results, sem = refs[:3], refs[3:6], refs[6]
    copies = [pltpu.make_async_copy(sources[i], results[i], sem.at[i]) for i in range(3)]
    for copy in copies:
        copy.start()
    for copy in copies:
        copy.wait()


def local(features, mask, labels, kernel_map, weight, classifier):
    vmem, anywhere = pl.BlockSpec(memory_space=pltpu.VMEM), pl.BlockSpec(memory_space=pl.ANY)
    shapes = [((512, 1024), BF16), ((1728, 64), F32), ((3, 64), F32)]
    results = pl.pallas_call(
        kernel,
        out_shape=[pltpu.VMEM(*shape) for shape in shapes],
        in_specs=[anywhere] * 6,
        out_specs=[vmem] * 3,
        scratch_shapes=[
            pltpu.VMEM((512, 1024), BF16),
            pltpu.VMEM((512, 16), I32),
            pltpu.VMEM((512, 16), I32),
            pltpu.SMEM((2, 27), I32),
            pltpu.VMEM((1728, 64), BF16),
            pltpu.VMEM((3, 64), BF16),
            pltpu.VMEM((2, 256, 1024), BF16),
            pltpu.VMEM((512, 1024), F32),
            pltpu.VMEM((2, 256, 1024), BF16),
            pltpu.VMEM((2, 256, 1024), BF16),
            pltpu.VMEM((2, 256, 1024), F32),
            pltpu.VMEM((2, 2, 2, 16, 1024), BF16),
            pltpu.VMEM((2, 4, 16, 128), BF16),
            pltpu.VMEM((4, 16, 128), F32),
            pltpu.VMEM((2, 2, 2, 16, 1024), BF16),
            pltpu.VMEM((2, 2, 2, 16, 1024), BF16),
            pltpu.VMEM((2, 4, 16, 128), BF16),
            pltpu.VMEM((3, 2, 288, 1152), BF16),
            pltpu.VMEM((3, 2, 288, 1152), BF16),
            pltpu.VMEM((2, 2, 24, 1152), F32),
            pltpu.VMEM((4, 128, 1152), BF16),
            pltpu.VMEM((2, 2, 16, 1024), F32),
            pltpu.VMEM((3456, 256), BF16),
            pltpu.VMEM((3456, 256), BF16),
            pltpu.VMEM((256, 2560), BF16),
            pltpu.VMEM((128, 1024), BF16),
            pltpu.VMEM((10, 64, 128), F32),
            pltpu.VMEM((14, 64, 128), BF16),
            pltpu.VMEM((16, 64, 128), BF16),
            pltpu.VMEM((8, 64, 128), BF16),
            pltpu.VMEM((14, 64, 128), BF16),
            pltpu.SemaphoreType.DMA((7,)),
            pltpu.SemaphoreType.DMA((56,)),
            pltpu.SemaphoreType.DMA((56,)),
        ],
        compiler_params=pltpu.CompilerParams(
            collective_id=0, has_side_effects=True, vmem_limit_bytes=40 * 1024 * 1024
        ),
        name="sparse_conv",
    )(
        *[
            pltpu.with_memory_space_constraint(x, pltpu.HBM)
            for x in (
                features.reshape(512, 1024),
                mask.reshape(512, 16),
                labels.reshape(512, 16),
                kernel_map.reshape(2, 27),
                weight.reshape(1728, 64),
                classifier,
            )
        ]
    )
    grad_input, wg, cg = pl.pallas_call(
        finish,
        out_shape=[pltpu.HBM(*shape) for shape in shapes],
        in_specs=[vmem] * 3,
        out_specs=[anywhere] * 3,
        scratch_shapes=[pltpu.SemaphoreType.DMA((3,))],
        name="finish",
    )(*[pltpu.with_memory_space_constraint(x, pltpu.VMEM) for x in results])
    return grad_input.reshape(1, 1, 2, 16, 16, 1024), wg.reshape(27, 64, 64), cg


def solution(mesh):
    in_specs = (
        P("gx", "gy", None, None, None, None),
        P("gx", "gy", None, None, None, None),
        P("gx", "gy", None, None, None, None),
        P("gx", "gy", None, None),
        P(),
        P(),
    )
    out_specs = (P("gx", "gy", None, None, None, None), P(), P())
    return jax.shard_map(local, mesh=mesh, in_specs=in_specs, out_specs=out_specs, check_vma=False)
```

```python
import jax
import jax.numpy as jnp
from jax import lax
from jax.experimental import pallas as pl
from jax.experimental.pallas import tpu as pltpu
from jax.sharding import PartitionSpec as P

MESH = pl.DeviceIdType.MESH
F32, BF16, I32 = jnp.float32, jnp.bfloat16, jnp.int32
NX, NY = 8, 16
CHUNKS = 14
OWNER = [t * 5 % NY for t in range(CHUNKS)]
PARTS = [(0, 4), (4, 9), (9, 14)]
WHOLE = [0, 1, 2, 4, 5, 6, 9, 10, 11]
PAIRS = [3, 7, 8, 12, 13]
DIRS = [(a, b) for a in (-1, 0, 1) for b in (-1, 0, 1) if (a, b) != (0, 0)]
XD = [(-1, 0), (1, 0)]
YD = [(0, -1), (0, 1)]
CD = [(-1, -1), (-1, 1), (1, -1), (1, 1)]


def iota(shape, dim):
    return lax.broadcasted_iota(I32, shape, dim)


def dot(a, b):
    return jnp.dot(a, b, preferred_element_type=F32)


def dot_t(a, b):
    return lax.dot_general(a, b, (((1,), (1,)), ((), ())), preferred_element_type=F32)


def tdot(a, b):
    return lax.dot_general(a, b, (((0,), (0,)), ((), ())), preferred_element_type=F32)


def one_hot(cond):
    return jnp.where(cond, 1.0, 0.0).astype(BF16)


def pick(m, first, second):
    return jnp.where(m == 0, first, jnp.where(m == 1, second, 0.0))


def low_half(rows):
    return iota((rows, 128), 1) < 64


def swap(x):
    return pltpu.roll(x, 64, axis=1)


def deepen(before, body, after):
    tiles = [before] + body + [after]
    low = low_half(before.shape[0])
    return [swap(jnp.where(low, tiles[k + 1], tiles[k])) for k in range(9)]


def offset_id(a, b, c):
    return (a + 1) * 9 + (b + 1) * 3 + (c + 1)


class Halo:
    def __init__(self, src, ysend, csend, corner, rx, ry, rc, send_sem, recv_sem, base, gx, gy):
        self.src, self.ysend, self.csend, self.corner = src, ysend, csend, corner
        self.rx, self.ry, self.rc = rx, ry, rc
        self.send_sem, self.recv_sem, self.base = send_sem, recv_sem, base
        self.gx, self.gy = gx, gy

    def prepare(self):
        r = iota((32, 256), 0)
        c = iota((32, 256), 1)
        sel = one_hot(c == (r & 15) * 16 + (r >> 4) * 15)
        for s in range(2):
            rows = dot(sel, self.src[s])
            self.ysend[0, s] = rows[:16].astype(BF16)
            self.ysend[1, s] = rows[16:].astype(BF16)
            for n, (a, b) in enumerate(CD):
                at = (16 if b > 0 else 0) + (15 if a > 0 else 0)
                for k in range(8):
                    self.corner[n, s * 8 + k : s * 8 + k + 1, :] = rows[at : at + 1, k * 128 : (k + 1) * 128]
        for n in range(4):
            self.csend[n] = self.corner[n].astype(BF16)

    def send(self):
        copies = self.copies()
        for copy in copies[:2]:
            copy.start()
        self.prepare()
        for copy in copies[2:]:
            copy.start()
        return copies

    def copies(self):
        out = []
        for n, (a, b) in enumerate(XD + YD + CD):
            if n < 2:
                src, dst, opp = self.src.at[:, pl.ds(15 * 16 if a > 0 else 0, 16), :], self.rx.at[1 - n], 1 - n
            elif n < 4:
                src, dst, opp = self.ysend.at[n - 2], self.ry.at[3 - n], 5 - n
            else:
                src, dst, opp = self.csend.at[n - 4], self.rc.at[7 - n], 11 - n
            to = (lax.rem(self.gx + a + NX, NX), lax.rem(self.gy + b + NY, NY))
            out.append(
                pltpu.make_async_remote_copy(
                    src_ref=src,
                    dst_ref=dst,
                    send_sem=self.send_sem.at[self.base + n],
                    recv_sem=self.recv_sem.at[self.base + opp],
                    device_id=to,
                    device_id_type=MESH,
                )
            )
        return out


def split_tiles(x):
    return [x[:, k * 128 : (k + 1) * 128] for k in range(x.shape[1] // 128)]


def spread_planes(tiles, low_row, high_row):
    rows = iota((16, 128), 0)
    down, up = [], []
    for k, t in enumerate(tiles):
        lanes = slice(k * 128, (k + 1) * 128)
        first = 0.0 if low_row is None else low_row[:, lanes]
        last = 0.0 if high_row is None else high_row[:, lanes]
        down.append(jnp.where(rows == 0, first, pltpu.roll(t, 1, axis=0)))
        up.append(jnp.where(rows == 15, last, pltpu.roll(t, 15, axis=0)))
    return down, tiles, up


def put(pad, s, plane, tiles, low_row=None, high_row=None):
    at = pl.multiple_of(plane * 16, 16)
    for dy, version in enumerate(spread_planes(tiles, low_row, high_row)):
        for k, t in enumerate(version):
            pad[dy, s, pl.ds(at, 16), k * 128 : (k + 1) * 128] = t.astype(BF16)


def from_slots(kmap, s, a, b, one, two):
    m = [kmap[s, offset_id(a, b, c)] for c in (-1, 0, 1)]
    return deepen(
        pick(m[0], one[:, 896:], two[:, 896:]),
        split_tiles(pick(m[1], one, two)),
        pick(m[2], one[:, :128], two[:, :128]),
    )


def own_tiles(src, kmap, s, x):
    rows = pl.ds(pl.multiple_of(x * 16, 16), 16)
    before = pick(kmap[s, 12], src[0, rows, 896:1024].astype(F32), src[1, rows, 896:1024].astype(F32))
    after = pick(kmap[s, 14], src[0, rows, 0:128].astype(F32), src[1, rows, 0:128].astype(F32))
    return deepen(before, split_tiles(src[s, rows, :].astype(F32)), after)


def corner_rows(halo, kmap, edge):
    low = low_half(8)
    for n, (a, b) in enumerate(CD):
        packed = halo.rc[n].astype(F32)
        e, w = (b + 1) // 2, (a + 1) // 2
        for s in range(2):
            m = [kmap[s, offset_id(a, b, c)] for c in (-1, 0, 1)]
            before, mid, after = (pick(v, packed[:8], packed[8:]) for v in m)
            prev = pltpu.roll(jnp.where(iota((8, 128), 0) == 7, before, mid), 1, axis=0)
            body = swap(jnp.where(low, mid, prev))
            last = swap(jnp.where(low, pltpu.roll(after, 7, axis=0), mid))
            for k in range(8):
                edge[e, s, 16 + w : 17 + w, k * 128 : (k + 1) * 128] = body[k : k + 1]
            edge[e, s, 16 + w : 17 + w, 1024:1152] = last[7:8]


def build_local(src, kmap, pad):
    for s in range(2):
        for dy in range(3):
            pad[dy, s, 0:16, :] = jnp.zeros((16, 1152), BF16)
            pad[dy, s, 272:288, :] = jnp.zeros((16, 1152), BF16)

        def plane(x, carry):
            put(pad, s, x + 1, own_tiles(src, kmap, s, x))
            return carry

        lax.fori_loop(0, 16, plane, 0, unroll=8)


def build_sides(halo, kmap, side, edge):
    corner_rows(halo, kmap, edge)
    for s in range(2):
        for w, (a, _) in enumerate(XD):
            tiles = from_slots(kmap, s, a, 0, halo.rx[w, 0].astype(F32), halo.rx[w, 1].astype(F32))
            versions = spread_planes(tiles, edge[0, s, 16 + w : 17 + w, :], edge[1, s, 16 + w : 17 + w, :])
            put_side(side, w, s, versions)
        for e, (_, b) in enumerate(YD):
            tiles = from_slots(kmap, s, 0, b, halo.ry[e, 0].astype(F32), halo.ry[e, 1].astype(F32))
            put_side(side, 2 + e, s, spread_planes(tiles, None, None))


def put_side(side, n, s, versions):
    for shift, tiles in enumerate(versions):
        cast = [t.astype(BF16) for t in tiles]
        for q in range(4):
            for k in range(3):
                at = (s * 4 + q) * 16
                lanes = shift * 384 + k * 128
                side[n, at : at + 16, lanes : lanes + 128] = cast[2 * q + k]


def add_sides(side, band, acc, beyond):
    for n in range(4):
        end = n % 2
        if n < 2:
            part = dot(side[n], band[end * 2304 : end * 2304 + 1152, :])
        else:
            at = [(dx * 3 + 2 * end) * 384 for dx in range(3)]
            part = dot(side[n], jnp.concatenate([band[i : i + 384, :] for i in at], axis=0))
        for s in range(2):
            for q in range(4):
                lanes = slice(q * 256, (q + 1) * 256)
                term = part[(s * 4 + q) * 16 : (s * 4 + q) * 16 + 16]
                if n < 2:
                    acc[s, 240 * end : 240 * end + 16, lanes] += term
                else:
                    beyond[end, s, :, lanes] = term


def build_padded(halo, kmap, pad, edge):
    corner_rows(halo, kmap, edge)
    for s in range(2):
        for e, (_, b) in enumerate(YD):
            tiles = from_slots(kmap, s, 0, b, halo.ry[e, 0].astype(F32), halo.ry[e, 1].astype(F32))
            edge[e, s, 0:16, :] = jnp.concatenate(tiles, axis=1)
        for w, (a, _) in enumerate(XD):
            tiles = from_slots(kmap, s, a, 0, halo.rx[w, 0].astype(F32), halo.rx[w, 1].astype(F32))
            put(pad, s, 17 * w, tiles, edge[0, s, 16 + w : 17 + w, :], edge[1, s, 16 + w : 17 + w, :])

        def plane(x, carry):
            put(pad, s, x + 1, own_tiles(halo.src, kmap, s, x), edge[0, s, pl.ds(x, 1), :], edge[1, s, pl.ds(x, 1), :])
            return carry

        lax.fori_loop(0, 16, plane, 0, unroll=8)


def conv(pad, band, qs):
    lanes = [pl.ds(pl.multiple_of(q * 256, 256), 384) for q in qs]
    pieces = [
        jnp.concatenate([pad[dy, s, pl.ds(dx * 16, 256), z] for z in lanes for s in range(2)], axis=0)
        for dx in range(3)
        for dy in range(3)
    ]
    return dot(jnp.concatenate(pieces, axis=1), band[...])


def build_band(wt, ref, turn):
    dup = one_hot((iota((64, 128), 1) & 63) == iota((64, 128), 0))
    low = low_half(64)
    zero = jnp.zeros((64, 128), F32)

    def group(g, carry):
        if turn:
            parts = [tdot(wt[pl.ds(pl.multiple_of((8 - g) * 192 + (2 - d) * 64, 64), 64), :], dup) for d in range(3)]
        else:
            fore = dot(wt[pl.ds(pl.multiple_of(g * 192, 64), 192), :], dup)
            parts = [fore[d * 64 : (d + 1) * 64] for d in range(3)]
        for i in range(6):
            for t in range(2):
                a, b = i - 2 * t, i - 2 * t - 1
                x = jnp.where(low, parts[a] if 0 <= a < 3 else zero, parts[b] if 0 <= b < 3 else zero)
                at = pl.multiple_of(g * 384 + i * 64, 64)
                ref[pl.ds(at, 64), t * 128 : (t + 1) * 128] = x.astype(BF16)
        return carry

    lax.fori_loop(0, 9, group, 0)


class Reduction:
    def __init__(self, gx, gy, mine, red, got, swapped, gath, send_sem, recv_sem):
        self.gx, self.gy, self.mine = gx, gy, mine
        self.red, self.got, self.swapped, self.gath = red, got, swapped, gath
        self.send_sem, self.recv_sem = send_sem, recv_sem

    def copy(self, src, dst, send, recv, device):
        return pltpu.make_async_remote_copy(
            src_ref=src,
            dst_ref=dst,
            send_sem=self.send_sem.at[send],
            recv_sem=self.recv_sem.at[recv],
            device_id=device,
            device_id_type=MESH,
        )

    def to_owner(self, t, source):
        return self.copy(self.red.at[t], self.got.at[source], 16 + t, 16 + source, (self.gx, OWNER[t]))

    def to_owners_beside(self, d, source):
        to = (lax.rem(self.gx + d, NX), self.gy)
        return self.copy(self.swapped.at[self.gx], self.swapped.at[source], 32 + d, 32 + source, to)

    def to_all(self, d, t):
        to = (self.gx, lax.rem(self.gy + d, NY))
        return self.copy(self.gath.at[t], self.gath.at[t], 40 + d, 40 + t, to)

    def owns(self, part):
        return (self.mine >= PARTS[part][0]) & (self.mine < PARTS[part][1])

    def scatter(self, part):
        for t in range(*PARTS[part]):

            @pl.when(self.gy != OWNER[t])
            def _():
                self.to_owner(t, self.gy).start()

    def across(self, part):
        @pl.when(self.owns(part))
        def _():
            total = self.red[self.mine].astype(F32)
            for d in range(1, NY):
                source = lax.rem(self.gy + d, NY)
                self.to_owner(0, source).wait_recv()
                total += self.got[source].astype(F32)
            self.swapped[self.gx] = total.astype(BF16)
            for d in range(1, NX):
                self.to_owners_beside(d, self.gx).start()

    def gather(self, part):
        @pl.when(self.owns(part))
        def _():
            for d in range(1, NX):
                self.to_owners_beside(d, lax.rem(self.gx + NX - d, NX)).wait_recv()
            total = self.swapped[0].astype(F32)
            for d in range(1, NX):
                total += self.swapped[d].astype(F32)
            self.gath[self.mine] = total.astype(BF16)
            for d in range(1, NY):
                self.to_all(d, self.mine).start()

    def wait_sums(self):
        for t in range(CHUNKS):

            @pl.when(self.gy != OWNER[t])
            def _():
                self.to_owner(t, self.gy).wait_send()
                self.to_all(1, t).wait_recv()

    def wait_sent(self):
        @pl.when(self.mine < CHUNKS)
        def _():
            for d in range(1, NX):
                self.to_owners_beside(d, self.gx).wait_send()
            for d in range(1, NY):
                self.to_all(d, self.mine).wait_send()


def kernel(
    feat_h, mask_h, lab_h, kmap_h, wt_h, cls_h, out, wg, cg,
    feat, mask, lab, kmap, wt, cls, src, on, grad, hid, slope, ysend, csend, corner, rx, ry, rc, pad, pad_g, edge, side, beyond,
    band, flip, head, head_t, keep, target, tail, red, got, swapped, gath, local_sem, send_sem, recv_sem,
):
    gx, gy = lax.axis_index("gx"), lax.axis_index("gy")
    half = [pl.ds(0, 256), pl.ds(256, 256)]
    loads = [
        pltpu.make_async_copy(a, b, local_sem.at[n])
        for n, (a, b) in enumerate(
            [(mask_h, mask)] + [(feat_h.at[h, :], feat.at[h, :]) for h in half] + [(kmap_h, kmap), (wt_h, wt), (cls_h, cls), (lab_h, lab)]
        )
    ]
    for load in loads:
        load.start()
    barrier = pltpu.get_barrier_semaphore()
    peers = [(lax.rem(gx + a + NX, NX), lax.rem(gy + b + NY, NY)) for a, b in CD]
    peers += [(gx, lax.rem(gy + d, NY)) for d in range(1, NY)]
    peers += [(lax.rem(gx + d, NX), gy) for d in range(1, NX)]
    for peer in peers:
        pl.semaphore_signal(barrier, inc=1, device_id=peer, device_id_type=MESH)

    spread = one_hot((iota((16, 1024), 1) >> 6) == iota((16, 1024), 0))

    def mask_rows(i, carry):
        at = pl.multiple_of(i * 64, 64)
        wide = dot(mask[pl.ds(at, 64), :].astype(F32).astype(BF16), spread)
        on[pl.ds(at, 64), :] = wide
        s, r = i // 4, pl.multiple_of((i % 4) * 64, 64)
        src[s, pl.ds(r, 64), :] = (feat[pl.ds(at, 64), :].astype(F32) * wide).astype(BF16)
        return carry

    loads[0].wait()
    loads[1].wait()
    lax.fori_loop(0, 4, mask_rows, 0)
    loads[2].wait()
    lax.fori_loop(4, 8, mask_rows, 0)
    fore = Halo(src, ysend.at[0], csend.at[0], corner, rx.at[0], ry.at[0], rc.at[0], send_sem, recv_sem, 0, gx, gy)
    pl.semaphore_wait(barrier, len(peers))
    fore_copies = fore.send()

    for load in loads[3:]:
        load.wait()
    build_band(wt, band, False)
    lane, row = iota((128, 1024), 1), iota((128, 1024), 0)
    repeat = one_hot((iota((64, 1024), 1) & 63) == iota((64, 1024), 0))
    kind_row = iota((128, 1), 0) >> 4
    kind_row = jnp.where(kind_row >= 6, kind_row - 6, jnp.where(kind_row >= 3, kind_row - 3, kind_row))
    wide_cls = dot(cls[...], repeat)
    diag = (lane >> 6) == (row & 15)
    classes = jnp.where(
        kind_row == 0, wide_cls[0:1], jnp.where(kind_row == 1, wide_cls[1:2], wide_cls[2:3])
    )
    wide_head = jnp.where(diag, classes, 0.0)
    head[...] = wide_head.astype(BF16)
    head_t[...] = wide_head.T.astype(BF16)
    narrow = one_hot(((iota((16, 128), 1) & 15) == iota((16, 128), 0)) & (iota((16, 128), 1) < 48))
    kind = (iota((512, 128), 1) >> 4).astype(F32)
    keep[...] = dot(mask[...].astype(F32).astype(BF16), narrow)
    target[...] = jnp.where(dot(lab[...].astype(F32).astype(BF16), narrow) == kind, 1.0, 0.0)
    build_local(src, kmap, pad)

    def fore_chunk(i, carry):
        pre = conv(pad, band, [2 * i, 2 * i + 1])
        for h in range(2):
            lanes = pl.ds(pl.multiple_of(i * 512 + h * 256, 256), 256)
            for s in range(2):
                slope[s, :, lanes] = pre[(h * 2 + s) * 256 : (h * 2 + s + 1) * 256]
        return carry

    lax.fori_loop(0, 2, fore_chunk, 0)

    for copy in fore_copies:
        copy.wait_recv()
    build_sides(fore, kmap, side, edge)
    add_sides(side, band, slope, beyond)

    def activate(i, carry):
        s, x = i // 16, i % 16
        rows = pl.ds(pl.multiple_of(x * 16, 16), 16)
        y = iota((8, 1024), 0)
        pre = slope[s, rows, :]
        first = pre[:8] + jnp.where(y == 0, beyond[0, s, pl.ds(x, 1), :], 0.0)
        last = pre[8:] + jnp.where(y == 7, beyond[1, s, pl.ds(x, 1), :], 0.0)
        pre = jnp.concatenate([first, last], axis=0)
        voxel = on[pl.ds(pl.multiple_of(i * 16, 16), 16), :]
        sig = 0.5 * jnp.tanh(0.5 * pre) + 0.5
        hid[s, rows, :] = (pre * sig * voxel).astype(BF16)
        slope[s, rows, :] = sig * (1.0 + pre * (1.0 - sig)) * voxel
        return carry

    lax.fori_loop(0, 32, activate, 0, unroll=2)
    grad_logits = []
    for s in range(2):
        rows = slice(s * 256, (s + 1) * 256)
        logits = dot(hid[s], head_t[...])
        second, third = pltpu.roll(logits, 112, axis=1), pltpu.roll(logits, 96, axis=1)
        top = jnp.maximum(logits, jnp.maximum(second, third))
        mine = jnp.exp(logits - top)
        prob = mine / (mine + jnp.exp(second - top) + jnp.exp(third - top))
        grad_logits.append(((prob - target[rows, :]) * keep[rows, :]).astype(BF16))
        for q in range(4):
            lanes = slice(q * 256, (q + 1) * 256)
            g = dot(grad_logits[s], head[:, lanes]) * slope[s, :, lanes]
            grad[s, :, lanes] = g.astype(BF16)

    back = Halo(grad, ysend.at[1], csend.at[1], corner, rx.at[1], ry.at[1], rc.at[1], send_sem, recv_sem, 8, gx, gy)
    back_copies = back.send()
    quarters = [(s, slice(q * 256, (q + 1) * 256)) for s in range(2) for q in range(4)]
    rims = [jnp.concatenate([grad[s, 240 * w : 240 * w + 16, z] for s, z in quarters], axis=0) for w in range(2)]
    rims += [jnp.concatenate([back.ysend[e, s, :, z] for s, z in quarters], axis=0) for e in range(2)]
    inner = [grad[s, :, z] for s, z in quarters]
    low = low_half(64)
    mine = lax.rem(gy * 13, NY)
    reduction = Reduction(gx, gy, mine, red, got, swapped, gath, send_sem, recv_sem)
    class_part = tdot(grad_logits[0], hid[0]) + tdot(grad_logits[1], hid[1])
    for k in range(3):
        part = jnp.where(diag[:16], class_part[k * 16 : (k + 1) * 16], 0.0)
        part = jnp.sum(part, axis=0, keepdims=True)
        total = part[:, 0:128]
        for t in range(1, 8):
            total += part[:, t * 128 : (t + 1) * 128]
        tail[9, k : k + 1, :] = total + swap(total)
    tail[9, 3:64, :] = jnp.zeros((61, 128), F32)
    for dx in range(3):
        rows = pl.ds(dx * 16, 256)
        for dy in range(3):
            lhs = [pad[dy, s, rows, q * 256 : q * 256 + 384] for s in range(2) for q in range(4)]
            rhs = list(inner)
            if dx != 1:
                lhs.append(side[dx // 2, :, dy * 384 : (dy + 1) * 384])
                rhs.append(rims[dx // 2])
            if dy != 1:
                lhs.append(side[2 + dy // 2, :, dx * 384 : (dx + 1) * 384])
                rhs.append(rims[2 + dy // 2])
            full = tdot(jnp.concatenate(lhs, axis=0), jnp.concatenate(rhs, axis=0))
            even = full[0:192, :128] + full[128:320, 128:]
            odd = full[64:256, :128] + full[192:384, 128:]
            half = jnp.where(low_half(192), even, odd)
            both = half + swap(half)
            red[WHOLE[dx * 3 + dy]] = jnp.where(low, both[0:64], both[64:128]).astype(BF16)
            tail[dx * 3 + dy] = both[128:192]
        for h in ((0,), (1, 2), (3, 4))[dx]:
            red[PAIRS[h]] = jnp.where(low, tail[2 * h], tail[2 * h + 1]).astype(BF16)
        reduction.scatter(dx)
    reduction.across(0)

    build_band(wt, flip, True)
    for copy in back_copies:
        copy.wait_recv()
    build_padded(back, kmap, pad_g, edge)

    reduction.across(1)

    def back_chunk(q, carry):
        lanes = pl.ds(pl.multiple_of(q * 256, 256), 256)
        out[:, lanes] = (conv(pad_g, flip, [q]) * on[:, lanes]).astype(BF16)
        return carry

    lax.fori_loop(0, 1, back_chunk, 0)
    reduction.across(2)
    reduction.gather(0)
    lax.fori_loop(1, 3, back_chunk, 0)
    reduction.gather(1)
    reduction.gather(2)
    lax.fori_loop(3, 4, back_chunk, 0)
    for copy in fore_copies + back_copies:
        copy.wait_send()
    reduction.wait_sums()
    scale = float(NX * NY * 2 * 16**3) ** -0.5
    for g in range(9):
        chunk = gath[WHOLE[g]].astype(F32) * scale
        wg[g * 192 : g * 192 + 64, :] = chunk[:, :64]
        wg[g * 192 + 64 : g * 192 + 128, :] = swap(chunk)[:, :64]
    for h in range(5):
        chunk = gath[PAIRS[h]].astype(F32) * scale
        wg[h * 384 + 128 : h * 384 + 192, :] = chunk[:, :64]
        if h < 4:
            wg[h * 384 + 320 : h * 384 + 384, :] = swap(chunk)[:, :64]
    cg[...] = swap(gath[13].astype(F32) * scale)[:3, :64]
    reduction.wait_sent()


def finish(*refs):
    sources, results, sem = refs[:3], refs[3:6], refs[6]
    copies = [pltpu.make_async_copy(sources[i], results[i], sem.at[i]) for i in range(3)]
    for copy in copies:
        copy.start()
    for copy in copies:
        copy.wait()


def local(features, mask, labels, kernel_map, weight, classifier):
    vmem, anywhere = pl.BlockSpec(memory_space=pltpu.VMEM), pl.BlockSpec(memory_space=pl.ANY)
    shapes = [((512, 1024), BF16), ((1728, 64), F32), ((3, 64), F32)]
    results = pl.pallas_call(
        kernel,
        out_shape=[pltpu.VMEM(*shape) for shape in shapes],
        in_specs=[anywhere] * 6,
        out_specs=[vmem] * 3,
        scratch_shapes=[
            pltpu.VMEM((512, 1024), BF16),
            pltpu.VMEM((512, 16), I32),
            pltpu.VMEM((512, 16), I32),
            pltpu.SMEM((2, 27), I32),
            pltpu.VMEM((1728, 64), BF16),
            pltpu.VMEM((3, 64), BF16),
            pltpu.VMEM((2, 256, 1024), BF16),
            pltpu.VMEM((512, 1024), F32),
            pltpu.VMEM((2, 256, 1024), BF16),
            pltpu.VMEM((2, 256, 1024), BF16),
            pltpu.VMEM((2, 256, 1024), F32),
            pltpu.VMEM((2, 2, 2, 16, 1024), BF16),
            pltpu.VMEM((2, 4, 16, 128), BF16),
            pltpu.VMEM((4, 16, 128), F32),
            pltpu.VMEM((2, 2, 2, 16, 1024), BF16),
            pltpu.VMEM((2, 2, 2, 16, 1024), BF16),
            pltpu.VMEM((2, 4, 16, 128), BF16),
            pltpu.VMEM((3, 2, 288, 1152), BF16),
            pltpu.VMEM((3, 2, 288, 1152), BF16),
            pltpu.VMEM((2, 2, 24, 1152), F32),
            pltpu.VMEM((4, 128, 1152), BF16),
            pltpu.VMEM((2, 2, 16, 1024), F32),
            pltpu.VMEM((3456, 256), BF16),
            pltpu.VMEM((3456, 256), BF16),
            pltpu.VMEM((128, 1024), BF16),
            pltpu.VMEM((1024, 128), BF16),
            pltpu.VMEM((512, 128), F32),
            pltpu.VMEM((512, 128), F32),
            pltpu.VMEM((10, 64, 128), F32),
            pltpu.VMEM((14, 64, 128), BF16),
            pltpu.VMEM((16, 64, 128), BF16),
            pltpu.VMEM((8, 64, 128), BF16),
            pltpu.VMEM((14, 64, 128), BF16),
            pltpu.SemaphoreType.DMA((11,)),
            pltpu.SemaphoreType.DMA((56,)),
            pltpu.SemaphoreType.DMA((56,)),
        ],
        compiler_params=pltpu.CompilerParams(
            collective_id=0, has_side_effects=True, vmem_limit_bytes=40 * 1024 * 1024
        ),
        name="sparse_conv",
    )(
        *[
            pltpu.with_memory_space_constraint(x, pltpu.HBM)
            for x in (
                features.reshape(512, 1024),
                mask.reshape(512, 16),
                labels.reshape(512, 16),
                kernel_map.reshape(2, 27),
                weight.reshape(1728, 64),
                classifier,
            )
        ]
    )
    grad_input, wg, cg = pl.pallas_call(
        finish,
        out_shape=[pltpu.HBM(*shape) for shape in shapes],
        in_specs=[vmem] * 3,
        out_specs=[anywhere] * 3,
        scratch_shapes=[pltpu.SemaphoreType.DMA((3,))],
        name="finish",
    )(*[pltpu.with_memory_space_constraint(x, pltpu.VMEM) for x in results])
    return grad_input.reshape(1, 1, 2, 16, 16, 1024), wg.reshape(27, 64, 64), cg


def solution(mesh):
    in_specs = (
        P("gx", "gy", None, None, None, None),
        P("gx", "gy", None, None, None, None),
        P("gx", "gy", None, None, None, None),
        P("gx", "gy", None, None),
        P(),
        P(),
    )
    out_specs = (P("gx", "gy", None, None, None, None), P(), P())
    return jax.shard_map(local, mesh=mesh, in_specs=in_specs, out_specs=out_specs, check_vma=False)
```

```python
import jax
import jax.numpy as jnp
from jax import lax
from jax.experimental import pallas as pl
from jax.experimental.pallas import tpu as pltpu
from jax.sharding import PartitionSpec as P

MESH = pl.DeviceIdType.MESH
F32, BF16, I32 = jnp.float32, jnp.bfloat16, jnp.int32
NX, NY = 8, 16
CHUNKS = 14
OWNER = [t * 5 % NY for t in range(CHUNKS)]
PARTS = [(0, 4), (4, 9), (9, 14)]
WHOLE = [0, 1, 2, 4, 5, 6, 9, 10, 11]
PAIRS = [3, 7, 8, 12, 13]
DIRS = [(a, b) for a in (-1, 0, 1) for b in (-1, 0, 1) if (a, b) != (0, 0)]
XD = [(-1, 0), (1, 0)]
YD = [(0, -1), (0, 1)]
CD = [(-1, -1), (-1, 1), (1, -1), (1, 1)]


def iota(shape, dim):
    return lax.broadcasted_iota(I32, shape, dim)


def dot(a, b):
    return jnp.dot(a, b, preferred_element_type=F32)


def dot_t(a, b):
    return lax.dot_general(a, b, (((1,), (1,)), ((), ())), preferred_element_type=F32)


def tdot(a, b):
    return lax.dot_general(a, b, (((0,), (0,)), ((), ())), preferred_element_type=F32)


def one_hot(cond):
    return jnp.where(cond, 1.0, 0.0).astype(BF16)


def pick(m, first, second):
    return jnp.where(m == 0, first, jnp.where(m == 1, second, 0.0))


def low_half(rows):
    return iota((rows, 128), 1) < 64


def swap(x):
    return pltpu.roll(x, 64, axis=1)


def deepen(before, body, after):
    tiles = [before] + body + [after]
    low = low_half(before.shape[0])
    return [swap(jnp.where(low, tiles[k + 1], tiles[k])) for k in range(9)]


def offset_id(a, b, c):
    return (a + 1) * 9 + (b + 1) * 3 + (c + 1)


class Halo:
    def __init__(self, src, ysend, csend, corner, rx, ry, rc, send_sem, recv_sem, base, gx, gy):
        self.src, self.ysend, self.csend, self.corner = src, ysend, csend, corner
        self.rx, self.ry, self.rc = rx, ry, rc
        self.send_sem, self.recv_sem, self.base = send_sem, recv_sem, base
        self.gx, self.gy = gx, gy

    def prepare(self):
        r = iota((32, 256), 0)
        c = iota((32, 256), 1)
        sel = one_hot(c == (r & 15) * 16 + (r >> 4) * 15)
        for s in range(2):
            rows = dot(sel, self.src[s])
            self.ysend[0, s] = rows[:16].astype(BF16)
            self.ysend[1, s] = rows[16:].astype(BF16)
            for n, (a, b) in enumerate(CD):
                at = (16 if b > 0 else 0) + (15 if a > 0 else 0)
                for k in range(8):
                    self.corner[n, s * 8 + k : s * 8 + k + 1, :] = rows[at : at + 1, k * 128 : (k + 1) * 128]
        for n in range(4):
            self.csend[n] = self.corner[n].astype(BF16)

    def send(self):
        copies = self.copies()
        for copy in copies[:2]:
            copy.start()
        self.prepare()
        for copy in copies[2:]:
            copy.start()
        return copies

    def copies(self):
        out = []
        for n, (a, b) in enumerate(XD + YD + CD):
            if n < 2:
                src, dst, opp = self.src.at[:, pl.ds(15 * 16 if a > 0 else 0, 16), :], self.rx.at[1 - n], 1 - n
            elif n < 4:
                src, dst, opp = self.ysend.at[n - 2], self.ry.at[3 - n], 5 - n
            else:
                src, dst, opp = self.csend.at[n - 4], self.rc.at[7 - n], 11 - n
            to = (lax.rem(self.gx + a + NX, NX), lax.rem(self.gy + b + NY, NY))
            out.append(
                pltpu.make_async_remote_copy(
                    src_ref=src,
                    dst_ref=dst,
                    send_sem=self.send_sem.at[self.base + n],
                    recv_sem=self.recv_sem.at[self.base + opp],
                    device_id=to,
                    device_id_type=MESH,
                )
            )
        return out


def split_tiles(x):
    return [x[:, k * 128 : (k + 1) * 128] for k in range(x.shape[1] // 128)]


def spread_planes(tiles, low_row, high_row):
    rows = iota((16, 128), 0)
    down, up = [], []
    for k, t in enumerate(tiles):
        lanes = slice(k * 128, (k + 1) * 128)
        first = 0.0 if low_row is None else low_row[:, lanes]
        last = 0.0 if high_row is None else high_row[:, lanes]
        down.append(jnp.where(rows == 0, first, pltpu.roll(t, 1, axis=0)))
        up.append(jnp.where(rows == 15, last, pltpu.roll(t, 15, axis=0)))
    return down, tiles, up


def put(pad, s, plane, tiles, low_row=None, high_row=None):
    at = pl.multiple_of(plane * 16, 16)
    for dy, version in enumerate(spread_planes(tiles, low_row, high_row)):
        for k, t in enumerate(version):
            pad[dy, s, pl.ds(at, 16), k * 128 : (k + 1) * 128] = t.astype(BF16)


def from_slots(kmap, s, a, b, one, two):
    m = [kmap[s, offset_id(a, b, c)] for c in (-1, 0, 1)]
    return deepen(
        pick(m[0], one[:, 896:], two[:, 896:]),
        split_tiles(pick(m[1], one, two)),
        pick(m[2], one[:, :128], two[:, :128]),
    )


def own_tiles(src, kmap, s, x):
    rows = pl.ds(pl.multiple_of(x * 16, 16), 16)
    before = pick(kmap[s, 12], src[0, rows, 896:1024].astype(F32), src[1, rows, 896:1024].astype(F32))
    after = pick(kmap[s, 14], src[0, rows, 0:128].astype(F32), src[1, rows, 0:128].astype(F32))
    return deepen(before, split_tiles(src[s, rows, :].astype(F32)), after)


def corner_rows(halo, kmap, edge):
    low = low_half(8)
    for n, (a, b) in enumerate(CD):
        packed = halo.rc[n].astype(F32)
        e, w = (b + 1) // 2, (a + 1) // 2
        for s in range(2):
            m = [kmap[s, offset_id(a, b, c)] for c in (-1, 0, 1)]
            before, mid, after = (pick(v, packed[:8], packed[8:]) for v in m)
            prev = pltpu.roll(jnp.where(iota((8, 128), 0) == 7, before, mid), 1, axis=0)
            body = swap(jnp.where(low, mid, prev))
            last = swap(jnp.where(low, pltpu.roll(after, 7, axis=0), mid))
            for k in range(8):
                edge[e, s, 16 + w : 17 + w, k * 128 : (k + 1) * 128] = body[k : k + 1]
            edge[e, s, 16 + w : 17 + w, 1024:1152] = last[7:8]


def build_local(src, kmap, pad):
    for s in range(2):
        for dy in range(3):
            pad[dy, s, 0:16, :] = jnp.zeros((16, 1152), BF16)
            pad[dy, s, 272:288, :] = jnp.zeros((16, 1152), BF16)

        def plane(x, carry):
            put(pad, s, x + 1, own_tiles(src, kmap, s, x))
            return carry

        lax.fori_loop(0, 16, plane, 0, unroll=8)


def build_sides(halo, kmap, side, edge):
    corner_rows(halo, kmap, edge)
    for s in range(2):
        for w, (a, _) in enumerate(XD):
            tiles = from_slots(kmap, s, a, 0, halo.rx[w, 0].astype(F32), halo.rx[w, 1].astype(F32))
            versions = spread_planes(tiles, edge[0, s, 16 + w : 17 + w, :], edge[1, s, 16 + w : 17 + w, :])
            put_side(side, w, s, versions)
        for e, (_, b) in enumerate(YD):
            tiles = from_slots(kmap, s, 0, b, halo.ry[e, 0].astype(F32), halo.ry[e, 1].astype(F32))
            put_side(side, 2 + e, s, spread_planes(tiles, None, None))


def put_side(side, n, s, versions):
    for shift, tiles in enumerate(versions):
        cast = [t.astype(BF16) for t in tiles]
        for q in range(4):
            for k in range(3):
                at = (s * 4 + q) * 16
                lanes = shift * 384 + k * 128
                side[n, at : at + 16, lanes : lanes + 128] = cast[2 * q + k]


def add_sides(side, band, acc, beyond):
    for n in range(4):
        end = n % 2
        if n < 2:
            part = dot(side[n], band[end * 2304 : end * 2304 + 1152, :])
        else:
            at = [(dx * 3 + 2 * end) * 384 for dx in range(3)]
            part = dot(side[n], jnp.concatenate([band[i : i + 384, :] for i in at], axis=0))
        for s in range(2):
            for q in range(4):
                lanes = slice(q * 256, (q + 1) * 256)
                term = part[(s * 4 + q) * 16 : (s * 4 + q) * 16 + 16]
                if n < 2:
                    acc[s, 240 * end : 240 * end + 16, lanes] += term
                else:
                    beyond[end, s, :, lanes] = term


def build_padded(halo, kmap, pad, edge):
    corner_rows(halo, kmap, edge)
    for s in range(2):
        for e, (_, b) in enumerate(YD):
            tiles = from_slots(kmap, s, 0, b, halo.ry[e, 0].astype(F32), halo.ry[e, 1].astype(F32))
            edge[e, s, 0:16, :] = jnp.concatenate(tiles, axis=1)
        for w, (a, _) in enumerate(XD):
            tiles = from_slots(kmap, s, a, 0, halo.rx[w, 0].astype(F32), halo.rx[w, 1].astype(F32))
            put(pad, s, 17 * w, tiles, edge[0, s, 16 + w : 17 + w, :], edge[1, s, 16 + w : 17 + w, :])

        def plane(x, carry):
            put(pad, s, x + 1, own_tiles(halo.src, kmap, s, x), edge[0, s, pl.ds(x, 1), :], edge[1, s, pl.ds(x, 1), :])
            return carry

        lax.fori_loop(0, 16, plane, 0, unroll=8)


def conv(pad, band, qs):
    lanes = [pl.ds(pl.multiple_of(q * 256, 256), 384) for q in qs]
    pieces = [
        jnp.concatenate([pad[dy, s, pl.ds(dx * 16, 256), z] for z in lanes for s in range(2)], axis=0)
        for dx in range(3)
        for dy in range(3)
    ]
    return dot(jnp.concatenate(pieces, axis=1), band[...])


def build_band(wt, ref, turn):
    dup = one_hot((iota((64, 128), 1) & 63) == iota((64, 128), 0))
    low = low_half(64)
    zero = jnp.zeros((64, 128), F32)

    def group(g, carry):
        if turn:
            parts = [tdot(wt[pl.ds(pl.multiple_of((8 - g) * 192 + (2 - d) * 64, 64), 64), :], dup) for d in range(3)]
        else:
            fore = dot(wt[pl.ds(pl.multiple_of(g * 192, 64), 192), :], dup)
            parts = [fore[d * 64 : (d + 1) * 64] for d in range(3)]
        for i in range(6):
            for t in range(2):
                a, b = i - 2 * t, i - 2 * t - 1
                x = jnp.where(low, parts[a] if 0 <= a < 3 else zero, parts[b] if 0 <= b < 3 else zero)
                at = pl.multiple_of(g * 384 + i * 64, 64)
                ref[pl.ds(at, 64), t * 128 : (t + 1) * 128] = x.astype(BF16)
        return carry

    lax.fori_loop(0, 9, group, 0)


class Reduction:
    def __init__(self, gx, gy, mine, red, got, swapped, gath, send_sem, recv_sem):
        self.gx, self.gy, self.mine = gx, gy, mine
        self.red, self.got, self.swapped, self.gath = red, got, swapped, gath
        self.send_sem, self.recv_sem = send_sem, recv_sem

    def copy(self, src, dst, send, recv, device):
        return pltpu.make_async_remote_copy(
            src_ref=src,
            dst_ref=dst,
            send_sem=self.send_sem.at[send],
            recv_sem=self.recv_sem.at[recv],
            device_id=device,
            device_id_type=MESH,
        )

    def to_owner(self, t, source):
        return self.copy(self.red.at[t], self.got.at[source], 16 + t, 16 + source, (self.gx, OWNER[t]))

    def to_owners_beside(self, d, source):
        to = (lax.rem(self.gx + d, NX), self.gy)
        return self.copy(self.swapped.at[self.gx], self.swapped.at[source], 32 + d, 32 + source, to)

    def to_all(self, d, t):
        to = (self.gx, lax.rem(self.gy + d, NY))
        return self.copy(self.gath.at[t], self.gath.at[t], 40 + d, 40 + t, to)

    def owns(self, part):
        return (self.mine >= PARTS[part][0]) & (self.mine < PARTS[part][1])

    def scatter(self, part):
        for t in range(*PARTS[part]):

            @pl.when(self.gy != OWNER[t])
            def _():
                self.to_owner(t, self.gy).start()

    def across(self, part):
        @pl.when(self.owns(part))
        def _():
            total = self.red[self.mine].astype(F32)
            for d in range(1, NY):
                source = lax.rem(self.gy + d, NY)
                self.to_owner(0, source).wait_recv()
                total += self.got[source].astype(F32)
            self.swapped[self.gx] = total.astype(BF16)
            for d in range(1, NX):
                self.to_owners_beside(d, self.gx).start()

    def gather(self, part):
        @pl.when(self.owns(part))
        def _():
            for d in range(1, NX):
                self.to_owners_beside(d, lax.rem(self.gx + NX - d, NX)).wait_recv()
            total = self.swapped[0].astype(F32)
            for d in range(1, NX):
                total += self.swapped[d].astype(F32)
            self.gath[self.mine] = total.astype(BF16)
            for d in range(1, NY):
                self.to_all(d, self.mine).start()

    def wait_sums(self):
        for t in range(CHUNKS):

            @pl.when(self.gy != OWNER[t])
            def _():
                self.to_owner(t, self.gy).wait_send()
                self.to_all(1, t).wait_recv()

    def wait_sent(self):
        @pl.when(self.mine < CHUNKS)
        def _():
            for d in range(1, NX):
                self.to_owners_beside(d, self.gx).wait_send()
            for d in range(1, NY):
                self.to_all(d, self.mine).wait_send()


def kernel(
    feat_h, mask_h, lab_h, kmap_h, wt_h, cls_h, out, wg, cg,
    feat, mask, lab, kmap, wt, cls, src, on, grad, hid, slope, ysend, csend, corner, rx, ry, rc, pad, pad_g, edge, side, beyond,
    band, flip, head, head_t, keep, target, tail, red, got, swapped, gath, local_sem, send_sem, recv_sem,
):
    gx, gy = lax.axis_index("gx"), lax.axis_index("gy")
    half = [pl.ds(0, 256), pl.ds(256, 256)]
    loads = [
        pltpu.make_async_copy(a, b, local_sem.at[n])
        for n, (a, b) in enumerate(
            [(mask_h, mask)] + [(feat_h.at[h, :], feat.at[h, :]) for h in half] + [(kmap_h, kmap), (wt_h, wt), (cls_h, cls), (lab_h, lab)]
        )
    ]
    for load in loads:
        load.start()
    barrier = pltpu.get_barrier_semaphore()
    peers = [(lax.rem(gx + a + NX, NX), lax.rem(gy + b + NY, NY)) for a, b in CD]
    peers += [(gx, lax.rem(gy + d, NY)) for d in range(1, NY)]
    peers += [(lax.rem(gx + d, NX), gy) for d in range(1, NX)]
    for peer in peers:
        pl.semaphore_signal(barrier, inc=1, device_id=peer, device_id_type=MESH)

    spread = one_hot((iota((16, 1024), 1) >> 6) == iota((16, 1024), 0))

    def mask_rows(i, carry):
        at = pl.multiple_of(i * 64, 64)
        wide = dot(mask[pl.ds(at, 64), :].astype(F32).astype(BF16), spread)
        on[pl.ds(at, 64), :] = wide
        s, r = i // 4, pl.multiple_of((i % 4) * 64, 64)
        src[s, pl.ds(r, 64), :] = (feat[pl.ds(at, 64), :].astype(F32) * wide).astype(BF16)
        return carry

    loads[0].wait()
    loads[1].wait()
    lax.fori_loop(0, 4, mask_rows, 0)
    loads[2].wait()
    lax.fori_loop(4, 8, mask_rows, 0)
    fore = Halo(src, ysend.at[0], csend.at[0], corner, rx.at[0], ry.at[0], rc.at[0], send_sem, recv_sem, 0, gx, gy)
    pl.semaphore_wait(barrier, len(peers))
    fore_copies = fore.send()

    for load in loads[3:]:
        load.wait()
    build_band(wt, band, False)
    lane, row = iota((128, 1024), 1), iota((128, 1024), 0)
    repeat = one_hot((iota((64, 1024), 1) & 63) == iota((64, 1024), 0))
    kind_row = iota((128, 1), 0) >> 4
    kind_row = jnp.where(kind_row >= 6, kind_row - 6, jnp.where(kind_row >= 3, kind_row - 3, kind_row))
    wide_cls = dot(cls[...], repeat)
    diag = (lane >> 6) == (row & 15)
    classes = jnp.where(
        kind_row == 0, wide_cls[0:1], jnp.where(kind_row == 1, wide_cls[1:2], wide_cls[2:3])
    )
    wide_head = jnp.where(diag, classes, 0.0)
    head[...] = wide_head.astype(BF16)
    head_t[...] = wide_head.T.astype(BF16)
    narrow = one_hot(((iota((16, 128), 1) & 15) == iota((16, 128), 0)) & (iota((16, 128), 1) < 48))
    kind = (iota((512, 128), 1) >> 4).astype(F32)
    keep[...] = dot(mask[...].astype(F32).astype(BF16), narrow)
    target[...] = jnp.where(dot(lab[...].astype(F32).astype(BF16), narrow) == kind, 1.0, 0.0)
    build_local(src, kmap, pad)

    def fore_chunk(i, carry):
        pre = conv(pad, band, [2 * i, 2 * i + 1])
        for h in range(2):
            lanes = pl.ds(pl.multiple_of(i * 512 + h * 256, 256), 256)
            for s in range(2):
                slope[s, :, lanes] = pre[(h * 2 + s) * 256 : (h * 2 + s + 1) * 256]
        return carry

    lax.fori_loop(0, 2, fore_chunk, 0)

    for copy in fore_copies:
        copy.wait_recv()
    build_sides(fore, kmap, side, edge)
    add_sides(side, band, slope, beyond)

    def activate(i, carry):
        s, x = i // 16, i % 16
        rows = pl.ds(pl.multiple_of(x * 16, 16), 16)
        y = iota((8, 1024), 0)
        pre = slope[s, rows, :]
        first = pre[:8] + jnp.where(y == 0, beyond[0, s, pl.ds(x, 1), :], 0.0)
        last = pre[8:] + jnp.where(y == 7, beyond[1, s, pl.ds(x, 1), :], 0.0)
        pre = jnp.concatenate([first, last], axis=0)
        voxel = on[pl.ds(pl.multiple_of(i * 16, 16), 16), :]
        sig = 0.5 * jnp.tanh(0.5 * pre) + 0.5
        hid[s, rows, :] = (pre * sig * voxel).astype(BF16)
        slope[s, rows, :] = sig * (1.0 + pre * (1.0 - sig)) * voxel
        return carry

    lax.fori_loop(0, 32, activate, 0, unroll=2)
    grad_logits = []
    for s in range(2):
        rows = slice(s * 256, (s + 1) * 256)
        logits = dot(hid[s], head_t[...])
        second, third = pltpu.roll(logits, 112, axis=1), pltpu.roll(logits, 96, axis=1)
        top = jnp.maximum(logits, jnp.maximum(second, third))
        mine = jnp.exp(logits - top)
        prob = mine / (mine + jnp.exp(second - top) + jnp.exp(third - top))
        grad_logits.append(((prob - target[rows, :]) * keep[rows, :]).astype(BF16))
        for q in range(4):
            lanes = slice(q * 256, (q + 1) * 256)
            g = dot(grad_logits[s], head[:, lanes]) * slope[s, :, lanes]
            grad[s, :, lanes] = g.astype(BF16)

    back = Halo(grad, ysend.at[1], csend.at[1], corner, rx.at[1], ry.at[1], rc.at[1], send_sem, recv_sem, 8, gx, gy)
    back_copies = back.send()
    quarters = [(s, slice(q * 256, (q + 1) * 256)) for s in range(2) for q in range(4)]
    rims = [jnp.concatenate([grad[s, 240 * w : 240 * w + 16, z] for s, z in quarters], axis=0) for w in range(2)]
    rims += [jnp.concatenate([back.ysend[e, s, :, z] for s, z in quarters], axis=0) for e in range(2)]
    inner = [grad[s, :, z] for s, z in quarters]
    low = low_half(64)
    mine = lax.rem(gy * 13, NY)
    reduction = Reduction(gx, gy, mine, red, got, swapped, gath, send_sem, recv_sem)
    class_part = tdot(grad_logits[0], hid[0]) + tdot(grad_logits[1], hid[1])
    for k in range(3):
        part = jnp.where(diag[:16], class_part[k * 16 : (k + 1) * 16], 0.0)
        part = jnp.sum(part, axis=0, keepdims=True)
        total = part[:, 0:128]
        for t in range(1, 8):
            total += part[:, t * 128 : (t + 1) * 128]
        tail[9, k : k + 1, :] = total + swap(total)
    tail[9, 3:64, :] = jnp.zeros((61, 128), F32)
    for dx in range(3):
        rows = pl.ds(dx * 16, 256)
        for dy in range(3):
            lhs = [pad[dy, s, rows, q * 256 : q * 256 + 384] for s in range(2) for q in range(4)]
            rhs = list(inner)
            if dx != 1:
                lhs.append(side[dx // 2, :, dy * 384 : (dy + 1) * 384])
                rhs.append(rims[dx // 2])
            if dy != 1:
                lhs.append(side[2 + dy // 2, :, dx * 384 : (dx + 1) * 384])
                rhs.append(rims[2 + dy // 2])
            full = tdot(jnp.concatenate(lhs, axis=0), jnp.concatenate(rhs, axis=0))
            even = full[0:192, :128] + full[128:320, 128:]
            odd = full[64:256, :128] + full[192:384, 128:]
            half = jnp.where(low_half(192), even, odd)
            both = half + swap(half)
            red[WHOLE[dx * 3 + dy]] = jnp.where(low, both[0:64], both[64:128]).astype(BF16)
            tail[dx * 3 + dy] = both[128:192]
        for h in ((0,), (1, 2), (3, 4))[dx]:
            red[PAIRS[h]] = jnp.where(low, tail[2 * h], tail[2 * h + 1]).astype(BF16)
        reduction.scatter(dx)
    reduction.across(0)

    build_band(wt, flip, True)
    for copy in back_copies:
        copy.wait_recv()
    reduction.across(1)
    build_padded(back, kmap, pad_g, edge)
    reduction.gather(0)


    def back_chunk(q, carry):
        lanes = pl.ds(pl.multiple_of(q * 256, 256), 256)
        out[:, lanes] = (conv(pad_g, flip, [q]) * on[:, lanes]).astype(BF16)
        return carry

    lax.fori_loop(0, 1, back_chunk, 0)
    reduction.across(2)
    lax.fori_loop(1, 3, back_chunk, 0)
    reduction.gather(1)
    reduction.gather(2)
    lax.fori_loop(3, 4, back_chunk, 0)
    for copy in fore_copies + back_copies:
        copy.wait_send()
    reduction.wait_sums()
    scale = float(NX * NY * 2 * 16**3) ** -0.5
    for g in range(9):
        chunk = gath[WHOLE[g]].astype(F32) * scale
        wg[g * 192 : g * 192 + 64, :] = chunk[:, :64]
        wg[g * 192 + 64 : g * 192 + 128, :] = swap(chunk)[:, :64]
    for h in range(5):
        chunk = gath[PAIRS[h]].astype(F32) * scale
        wg[h * 384 + 128 : h * 384 + 192, :] = chunk[:, :64]
        if h < 4:
            wg[h * 384 + 320 : h * 384 + 384, :] = swap(chunk)[:, :64]
    cg[...] = swap(gath[13].astype(F32) * scale)[:3, :64]
    reduction.wait_sent()


def finish(*refs):
    sources, results, sem = refs[:3], refs[3:6], refs[6]
    copies = [pltpu.make_async_copy(sources[i], results[i], sem.at[i]) for i in range(3)]
    for copy in copies:
        copy.start()
    for copy in copies:
        copy.wait()


def local(features, mask, labels, kernel_map, weight, classifier):
    vmem, anywhere = pl.BlockSpec(memory_space=pltpu.VMEM), pl.BlockSpec(memory_space=pl.ANY)
    shapes = [((512, 1024), BF16), ((1728, 64), F32), ((3, 64), F32)]
    results = pl.pallas_call(
        kernel,
        out_shape=[pltpu.VMEM(*shape) for shape in shapes],
        in_specs=[anywhere] * 6,
        out_specs=[vmem] * 3,
        scratch_shapes=[
            pltpu.VMEM((512, 1024), BF16),
            pltpu.VMEM((512, 16), I32),
            pltpu.VMEM((512, 16), I32),
            pltpu.SMEM((2, 27), I32),
            pltpu.VMEM((1728, 64), BF16),
            pltpu.VMEM((3, 64), BF16),
            pltpu.VMEM((2, 256, 1024), BF16),
            pltpu.VMEM((512, 1024), F32),
            pltpu.VMEM((2, 256, 1024), BF16),
            pltpu.VMEM((2, 256, 1024), BF16),
            pltpu.VMEM((2, 256, 1024), F32),
            pltpu.VMEM((2, 2, 2, 16, 1024), BF16),
            pltpu.VMEM((2, 4, 16, 128), BF16),
            pltpu.VMEM((4, 16, 128), F32),
            pltpu.VMEM((2, 2, 2, 16, 1024), BF16),
            pltpu.VMEM((2, 2, 2, 16, 1024), BF16),
            pltpu.VMEM((2, 4, 16, 128), BF16),
            pltpu.VMEM((3, 2, 288, 1152), BF16),
            pltpu.VMEM((3, 2, 288, 1152), BF16),
            pltpu.VMEM((2, 2, 24, 1152), F32),
            pltpu.VMEM((4, 128, 1152), BF16),
            pltpu.VMEM((2, 2, 16, 1024), F32),
            pltpu.VMEM((3456, 256), BF16),
            pltpu.VMEM((3456, 256), BF16),
            pltpu.VMEM((128, 1024), BF16),
            pltpu.VMEM((1024, 128), BF16),
            pltpu.VMEM((512, 128), F32),
            pltpu.VMEM((512, 128), F32),
            pltpu.VMEM((10, 64, 128), F32),
            pltpu.VMEM((14, 64, 128), BF16),
            pltpu.VMEM((16, 64, 128), BF16),
            pltpu.VMEM((8, 64, 128), BF16),
            pltpu.VMEM((14, 64, 128), BF16),
            pltpu.SemaphoreType.DMA((11,)),
            pltpu.SemaphoreType.DMA((56,)),
            pltpu.SemaphoreType.DMA((56,)),
        ],
        compiler_params=pltpu.CompilerParams(
            collective_id=0, has_side_effects=True, vmem_limit_bytes=40 * 1024 * 1024
        ),
        name="sparse_conv",
    )(
        *[
            pltpu.with_memory_space_constraint(x, pltpu.HBM)
            for x in (
                features.reshape(512, 1024),
                mask.reshape(512, 16),
                labels.reshape(512, 16),
                kernel_map.reshape(2, 27),
                weight.reshape(1728, 64),
                classifier,
            )
        ]
    )
    grad_input, wg, cg = pl.pallas_call(
        finish,
        out_shape=[pltpu.HBM(*shape) for shape in shapes],
        in_specs=[vmem] * 3,
        out_specs=[anywhere] * 3,
        scratch_shapes=[pltpu.SemaphoreType.DMA((3,))],
        name="finish",
    )(*[pltpu.with_memory_space_constraint(x, pltpu.VMEM) for x in results])
    return grad_input.reshape(1, 1, 2, 16, 16, 1024), wg.reshape(27, 64, 64), cg


def solution(mesh):
    in_specs = (
        P("gx", "gy", None, None, None, None),
        P("gx", "gy", None, None, None, None),
        P("gx", "gy", None, None, None, None),
        P("gx", "gy", None, None),
        P(),
        P(),
    )
    out_specs = (P("gx", "gy", None, None, None, None), P(), P())
    return jax.shard_map(local, mesh=mesh, in_specs=in_specs, out_specs=out_specs, check_vma=False)
```
